32 devices in a mesh: groups: 2 (over y), emit: 4 (over z), recv: 4 (over x, core).
Axes of the slice: x: 2, y: 2, z: 4, core: 2. Of those that a mesh axis runs over, the one named last changes fastest.
Arguments:
- positions: float32 [3, 8192], P(None, ('groups', 'emit', 'recv')), parts along dimension 1, may hold values from 0 to 1
- angles: float32 [2, 8192], P(None, ('groups', 'emit', 'recv')), parts along dimension 1, may hold values from -3.140625 to 3.140625
- areas: float32 [8192], P(('groups', 'emit', 'recv')), parts along dimension 0, may hold values from 0.00024414062 to 0.00390625
- emissivity: float32 [8192], P(('groups', 'emit', 'recv')), parts along dimension 0, may hold values from 0.1 to 0.9
- emission: float32 [32, 8192], P(None, ('groups', 'emit', 'recv')), parts along dimension 1, may hold values from 0.5 to 2
- radiosity_in: float32 [32, 8192], P(None, ('groups', 'emit', 'recv')), parts along dimension 1, may hold values from 0.2 to 2
- adjoint_in: float32 [32, 8192], P(None, ('groups', 'emit', 'recv')), parts along dimension 1, may hold values from 0 to 1.5
- visibility: int32 [64, 32], P(('groups', 'emit')), parts along dimension 0, may hold values 0 or 1
- inlet_patches: int32 [4096], P('groups'), parts along dimension 0, may hold values from 0 to 4095
- inlet_weights: float32 [32, 4096], P(None, 'groups'), parts along dimension 1, may hold values from 0.5 to 2
Outputs:
- radiosity_out: float32 [32, 8192], P(None, ('groups', 'emit', 'recv')), parts along dimension 1
- adjoint_out: float32 [32, 8192], P(None, ('groups', 'emit', 'recv')), parts along dimension 1
- emissivity_grad: float32 [8192], P(('groups', 'emit', 'recv')), parts along dimension 0
The draws below stay inside these ranges and needn't reach their ends.
There are 2 independent parts, one for each index of `groups`. The reference program is written for one: setup_inputs(seed, part) draws one part's arguments, and reference() takes and returns one part's arrays. A program takes and returns all parts, laid end to end along the dimension named above; each array names one. Nothing has to cross between parts.
Inputs may be any that keep to these rules, and one draw needn't show every extreme that they name: `inlet_patches`: an inlet patch may be listed more than once.
All inputs are finite; a program needn't handle non-finite values. No bound on the sum of `visibility` on one device may be relied on, other than what follows from the above.
Results may differ from the reference program's by a relative error of at most 0.0003.
Values may be sent and summed in bfloat16 or wider, within the bound.
A program may use at most 64 MiB of HBM per device.

```python
import math
import jax
import jax.numpy as jnp
from jax import lax

BLK = 128
CASES = 32
M_IN = 2048
NPATCH = 4096
NB = 32


def with_ends(entries, key, least, high):
    spot = [jax.random.randint(jax.random.fold_in(key, axis), (), 0, length) for axis, length in enumerate(entries.shape)]
    main_axis = entries.shape.index(max(entries.shape))
    next_to = spot[:main_axis] + [(spot[main_axis] + 1) % entries.shape[main_axis]] + spot[main_axis + 1:]
    return entries.at[tuple(spot)].set(least).at[tuple(next_to)].set(high)


def block_levels(rng, extent, shards, low, largest):
    factor_of, own = 1.0, jax.random.fold_in(rng, 6)
    for dim, blocks in shards:
        draws = jnp.exp(jax.random.uniform(jax.random.fold_in(own, dim), (blocks,), jnp.float32, low / len(shards), largest / len(shards)))
        factor_of = factor_of * jnp.repeat(draws, extent[dim] // blocks).reshape([-1 if axis == dim else 1 for axis in range(len(extent))])
    return factor_of


def setup_inputs(seed: int = 0, part: int = 0) -> dict:
    splits = jax.random.split(jax.random.key(seed), 11)
    part_keys = jax.random.split(jax.random.fold_in(splits[10], part), 11)
    positions = jnp.clip(1.0 * jax.random.uniform(part_keys[0], (3, NPATCH), jnp.float32) ** block_levels(part_keys[0], (3, NPATCH), ((1, 16),), -0.2, 0.2), 0.0, 1.0)
    angles = jnp.clip(jax.random.uniform(part_keys[1], (2, NPATCH), jnp.float32, -3.140625, 3.140625), -3.140625, 3.140625)
    areas = jnp.clip(jnp.exp(math.log(0.00390625) - 2.7725887 * jax.random.uniform(part_keys[2], (NPATCH,), jnp.float32) ** block_levels(part_keys[2], (NPATCH,), ((0, 16),), -0.2, 0.2)), 0.00024414062, 0.00390625)
    emissivity = jnp.clip(0.1 + 0.79999997 * jax.random.uniform(part_keys[3], (NPATCH,), jnp.float32) ** block_levels(part_keys[3], (NPATCH,), ((0, 16),), -0.2, 0.2), 0.1, 0.9)
    emission = jnp.clip(0.5 + 1.5 * jax.random.uniform(part_keys[4], (CASES, NPATCH), jnp.float32) ** block_levels(part_keys[4], (CASES, NPATCH), ((1, 16),), -0.2, 0.2), 0.5, 2.0)
    radiosity_in = jnp.clip(0.2 + 1.8 * jax.random.uniform(part_keys[5], (CASES, NPATCH), jnp.float32) ** block_levels(part_keys[5], (CASES, NPATCH), ((1, 16),), -0.2, 0.2), 0.2, 2.0)
    adjoint_in = jnp.clip(1.5 * jax.random.uniform(part_keys[6], (CASES, NPATCH), jnp.float32) ** block_levels(part_keys[6], (CASES, NPATCH), ((1, 16),), -0.2, 0.2), 0.0, 1.5)
    visibility = with_ends((jax.random.randint(part_keys[7], (NB, NB), 0, 4) < 3).astype(jnp.int32), jax.random.fold_in(part_keys[7], 1), 0, 1)
    inlet_patches = with_ends(jax.random.randint(part_keys[8], (M_IN,), 0, NPATCH), jax.random.fold_in(part_keys[8], 1), 0, NPATCH - 1).astype(jnp.int32)
    inlet_weights = jnp.clip(jax.random.uniform(part_keys[9], (CASES, M_IN), jnp.float32, 0.5, 2.0), 0.5, 2.0)
    return {"positions": positions, "angles": angles, "areas": areas, "emissivity": emissivity, "emission": emission, "radiosity_in": radiosity_in, "adjoint_in": adjoint_in, "visibility": visibility, "inlet_patches": inlet_patches, "inlet_weights": inlet_weights}


def patch_geometry(positions, angles, areas):
    polar = angles[0]
    azimuth = angles[1]
    normal = jnp.stack([jnp.sin(polar) * jnp.cos(azimuth), jnp.sin(polar) * jnp.sin(azimuth), jnp.cos(polar)])
    return jnp.concatenate([positions, normal, areas[None, :]], axis=0)


def view_tile(row_geom, col_geom, block_mask):
    delta_x = col_geom[0][None, :] - row_geom[0][:, None]
    delta_y = col_geom[1][None, :] - row_geom[1][:, None]
    delta_z = col_geom[2][None, :] - row_geom[2][:, None]
    dist_sq = delta_x * delta_x + delta_y * delta_y + delta_z * delta_z
    cos_emit = jnp.maximum(row_geom[3][:, None] * delta_x + row_geom[4][:, None] * delta_y + row_geom[5][:, None] * delta_z, 0.0)
    cos_recv = jnp.maximum(-(col_geom[3][None, :] * delta_x + col_geom[4][None, :] * delta_y + col_geom[5][None, :] * delta_z), 0.0)
    patch_area = row_geom[6][:, None]
    spread = dist_sq + patch_area
    kernel = cos_emit * cos_recv * patch_area / (math.pi * spread * spread)
    row_blocks, col_blocks = block_mask.shape
    rows_total = row_geom.shape[1]
    cols_total = col_geom.shape[1]
    expanded = jnp.broadcast_to(block_mask[:, None, :, None], (row_blocks, rows_total // row_blocks, col_blocks, cols_total // col_blocks)).reshape(rows_total, cols_total)
    return (expanded * kernel).astype(jnp.bfloat16)


def reference(positions, angles, areas, emissivity, emission, radiosity_in, adjoint_in, visibility, inlet_patches, inlet_weights):
    geometry = patch_geometry(positions, angles, areas)
    reflect = 1.0 - emissivity
    weighted = lax.optimization_barrier((reflect[None, :] * adjoint_in).astype(jnp.bfloat16)).astype(jnp.float32)
    values = lax.optimization_barrier(radiosity_in.astype(jnp.bfloat16)).astype(jnp.float32)
    full_mask = visibility.astype(jnp.float32)
    step_rows = 256
    block_count = NPATCH // step_rows

    def sweep_rows(forward, number):
        first = (number * step_rows).astype(jnp.int32)
        row_geom = lax.dynamic_slice_in_dim(geometry, first, step_rows, 1)
        mask_part = lax.dynamic_slice_in_dim(full_mask, first // BLK, step_rows // BLK, 0)
        tile = lax.optimization_barrier(view_tile(row_geom, geometry, mask_part)).astype(jnp.float32)
        value_part = lax.dynamic_slice_in_dim(values, first, step_rows, 1)
        forward = forward + jnp.dot(value_part, tile, precision=lax.Precision.HIGHEST, preferred_element_type=jnp.float32)
        adjoint_part = jnp.dot(weighted, tile.T, precision=lax.Precision.HIGHEST, preferred_element_type=jnp.float32)
        return forward, adjoint_part

    start_state = jnp.zeros((CASES, NPATCH), jnp.float32)
    incoming, pieces = lax.scan(sweep_rows, start_state, jnp.arange(block_count, dtype=jnp.int32))
    returned = jnp.transpose(pieces, (1, 0, 2)).reshape(CASES, NPATCH)
    source = jnp.zeros((CASES, NPATCH), jnp.float32).at[:, inlet_patches].add(inlet_weights)
    radiosity_out = emissivity[None, :] * emission + reflect[None, :] * incoming
    adjoint_out = source + returned
    emissivity_grad = jnp.sum(adjoint_out * (emission - incoming), axis=0)
    return (radiosity_out, adjoint_out, emissivity_grad)
```

```python
import functools
import math

import jax
import jax.numpy as jnp
from jax import lax
from jax.experimental import pallas as pl
from jax.experimental.pallas import tpu as pltpu
from jax.sharding import PartitionSpec as P

BLK = 128
MESH = pl.DeviceIdType.MESH
F32 = jnp.float32
BF16 = jnp.bfloat16


def flip(index, number):
    bit = 1
    while bit <= number:
        if number & bit:
            index = index + bit * (1 - 2 * ((index // bit) % 2))
        bit *= 2
    return index


def partner(index, number, count):
    if count & (count - 1) == 0:
        return flip(index, number)
    return lax.rem(index + number, count)


def split3(x):
    one = x.astype(BF16).astype(F32)
    rest = x - one
    two = rest.astype(BF16).astype(F32)
    return one, two, rest - two


def row_stack(x):
    one, two, three = split3(x)
    return jnp.concatenate([one, one, two, two, one, three], axis=0)


def col_stack(x):
    one, two, three = split3(x)
    return jnp.concatenate([one, two, one, two, three, one], axis=0)


def dot(a, b, ca, cb):
    return lax.dot_general(a, b, (((ca,), (cb,)), ((), ())), preferred_element_type=F32)


def emitter_forms(geom):
    q, normal, area = geom[0:3], geom[3:6], geom[6:7]
    zero = jnp.zeros_like(area)
    one = jnp.ones_like(area)
    scale = area * (1.0 / math.pi)
    scaled = normal * scale
    offset = -jnp.sum(scaled * q, axis=0, keepdims=True)
    square = jnp.sum(q * q, axis=0, keepdims=True) + area
    cos_emit = jnp.concatenate([scaled, offset, zero, zero, zero, zero], axis=0)
    cos_recv = jnp.concatenate([q, one, zero, zero, zero, zero], axis=0)
    spread = jnp.concatenate([-2.0 * q, square, one, zero, zero, zero], axis=0)
    return cos_emit, cos_recv, spread


def receiver_forms(geom):
    q, normal, area = geom[0:3], geom[3:6], geom[6:7]
    zero = jnp.zeros_like(area)
    one = jnp.ones_like(area)
    offset = -jnp.sum(normal * q, axis=0, keepdims=True)
    square = jnp.sum(q * q, axis=0, keepdims=True)
    cos_emit = jnp.concatenate([q, one, zero, zero, zero, zero], axis=0)
    cos_recv = jnp.concatenate([normal, offset, zero, zero, zero, zero], axis=0)
    spread = jnp.concatenate([q, one, square, zero, zero, zero], axis=0)
    return cos_emit, cos_recv, spread


def sweep(
    emit_count,
    recv_count,
    pos_ref,
    ang_ref,
    area_ref,
    emis_ref,
    emission_ref,
    rad_ref,
    adj_ref,
    vis_ref,
    inlet_ref,
    weight_ref,
    out_rad,
    out_adj,
    out_grad,
    row_geom,
    col_geom,
    row_val,
    col_wt,
    mask,
    form_a,
    form_b,
    form_s,
    fwd_part,
    fwd_got,
    adj_part,
    adj_got,
    geom_row_send,
    geom_row_recv,
    geom_col_send,
    geom_col_recv,
    val_send,
    val_recv,
    wt_send,
    wt_recv,
    fwd_send,
    fwd_recv,
    ret_send,
    ret_recv,
):
    e = lax.axis_index("emit")
    r = lax.axis_index("recv")
    own = pos_ref.shape[1]
    blocks = own // BLK
    row_total = own * recv_count

    barrier = pltpu.get_barrier_semaphore()
    for k in range(1, recv_count):
        pl.semaphore_signal(
            barrier, inc=1, device_id={"recv": partner(r, k, recv_count)}, device_id_type=MESH
        )
    for k in range(1, emit_count):
        pl.semaphore_signal(
            barrier, inc=1, device_id={"emit": partner(e, k, emit_count)}, device_id_type=MESH
        )

    q = pos_ref[...] - 0.5
    angles = ang_ref[...]
    sines = jnp.sin(angles)
    cosines = jnp.cos(angles)
    geometry = jnp.concatenate(
        [
            q,
            sines[0:1] * cosines[1:2],
            sines[0:1] * sines[1:2],
            cosines[0:1],
            area_ref[...],
            jnp.zeros((1, own), F32),
        ],
        axis=0,
    )
    row_geom[r] = geometry
    col_geom[e] = geometry
    reflect = 1.0 - emis_ref[...]
    row_val[r] = rad_ref[...].astype(BF16)
    col_wt[e] = (reflect * adj_ref[...]).astype(BF16)

    pl.semaphore_wait(barrier, recv_count + emit_count - 2)

    def copies(buf, dst, send, recv, axis, me, count, gather):
        out = []
        for k in range(1, count):
            peer = partner(me, k, count)
            out.append(
                pltpu.make_async_remote_copy(
                    src_ref=buf.at[me if gather else peer],
                    dst_ref=dst.at[me],
                    send_sem=send.at[peer],
                    recv_sem=recv.at[me],
                    device_id={axis: peer},
                    device_id_type=MESH,
                )
            )
        return out

    def arrival(dst, send, recv, axis, peer):
        return pltpu.make_async_remote_copy(
            src_ref=dst.at[peer],
            dst_ref=dst.at[peer],
            send_sem=send.at[peer],
            recv_sem=recv.at[peer],
            device_id={axis: peer},
            device_id_type=MESH,
        )

    row_geom_out = copies(row_geom, row_geom, geom_row_send, geom_row_recv, "recv", r, recv_count, True)
    col_geom_out = copies(col_geom, col_geom, geom_col_send, geom_col_recv, "emit", e, emit_count, True)
    val_out = copies(row_val, row_val, val_send, val_recv, "recv", r, recv_count, True)
    wt_out = copies(col_wt, col_wt, wt_send, wt_recv, "emit", e, emit_count, True)
    for copy in col_geom_out + row_geom_out + wt_out + val_out:
        copy.start()

    patch = (e * recv_count + r) * own + lax.broadcasted_iota(jnp.int32, (own, 1), 0)
    selector = jnp.where(inlet_ref[...] == patch, 1.0, 0.0).astype(BF16)
    weights = weight_ref[...]
    high = weights.astype(BF16)
    low = (weights - high.astype(F32)).astype(BF16)
    out_adj[...] = dot(high, selector, 1, 1) + dot(low, selector, 1, 1)

    all_blocks = vis_ref.shape[1]
    col_blocks = emit_count * blocks
    number = lax.broadcasted_iota(jnp.int32, (col_blocks, all_blocks), 0)
    wanted = (lax.div(number, blocks) * recv_count + r) * blocks + lax.rem(number, blocks)
    chosen = (lax.broadcasted_iota(jnp.int32, (col_blocks, all_blocks), 1) == wanted).astype(F32)
    tile_mask = dot(chosen.astype(BF16), vis_ref[...].astype(F32).astype(BF16), 1, 1)
    row_blocks = recv_count * blocks
    spot = lax.broadcasted_iota(jnp.int32, (row_blocks, row_total), 1) // BLK
    expand = (lax.broadcasted_iota(jnp.int32, (row_blocks, row_total), 0) == spot).astype(F32)
    mask[...] = dot(tile_mask.astype(BF16), expand.astype(BF16), 1, 0)

    for k in range(recv_count):
        peer = partner(r, k, recv_count)
        if k:
            arrival(row_geom, geom_row_send, geom_row_recv, "recv", peer).wait_recv()
        for form, buf in zip(emitter_forms(row_geom[peer]), (form_a, form_b, form_s)):
            buf[peer] = row_stack(form).astype(BF16)

    for k in range(recv_count):
        adj_part[k] = jnp.zeros(adj_part.shape[1:], F32)

    lane = lax.broadcasted_iota(jnp.int32, (1, own), 1) // BLK

    def columns(peer):
        forms = [col_stack(form) for form in receiver_forms(col_geom[peer])]
        spaced = jnp.concatenate([jnp.where(lane == b, forms[0], 0.0) for b in range(blocks)], axis=0)
        side_a = spaced.T.astype(BF16)
        side_b = forms[1].T.astype(BF16)
        side_s = forms[2].T.astype(BF16)
        weight = col_wt[peer]

        def rows(number, total):
            start = pl.multiple_of(number * own, own)
            base = form_a[number]
            masked = jnp.concatenate(
                [
                    base * mask[pl.ds(peer * blocks + b, 1), pl.ds(start, own)].astype(BF16)
                    for b in range(blocks)
                ],
                axis=0,
            )
            cos_emit = jnp.maximum(dot(side_a, masked, 1, 0), 0.0)
            cos_recv = jnp.maximum(dot(side_b, form_b[number], 1, 0), 0.0)
            spread = dot(side_s, form_s[number], 1, 0)
            tile = (cos_emit * cos_recv * pl.reciprocal(spread * spread, approx=True)).astype(BF16)
            adj_part[number] += dot(weight, tile, 1, 0)
            return total + dot(row_val[number], tile, 1, 1)

        zero = jnp.zeros(fwd_part.shape[1:], F32)
        fwd_part[peer] = lax.fori_loop(0, recv_count, rows, zero, unroll=recv_count <= 4)

    for k in range(1, recv_count):
        arrival(row_val, val_send, val_recv, "recv", partner(r, k, recv_count)).wait_recv()

    fwd_out = copies(fwd_part, fwd_got, fwd_send, fwd_recv, "emit", e, emit_count, False)
    columns(e)
    for k in reversed(range(1, emit_count)):
        peer = partner(e, k, emit_count)
        arrival(col_geom, geom_col_send, geom_col_recv, "emit", peer).wait_recv()
        arrival(col_wt, wt_send, wt_recv, "emit", peer).wait_recv()
        columns(peer)
        fwd_out[k - 1].start()

    ret_out = copies(adj_part, adj_got, ret_send, ret_recv, "recv", r, recv_count, False)
    for copy in ret_out:
        copy.start()

    incoming = fwd_part[e]
    for k in range(1, emit_count):
        peer = partner(e, k, emit_count)
        arrival(fwd_got, fwd_send, fwd_recv, "emit", peer).wait_recv()
        incoming = incoming + fwd_got[peer]
    emission = emission_ref[...]
    out_rad[...] = emis_ref[...] * emission + reflect * incoming
    adjoint = out_adj[...] + adj_part[r]
    for k in range(1, recv_count):
        peer = partner(r, k, recv_count)
        arrival(adj_got, ret_send, ret_recv, "recv", peer).wait_recv()
        adjoint = adjoint + adj_got[peer]
    out_adj[...] = adjoint
    out_grad[...] = jnp.sum(adjoint * (emission - incoming), axis=0, keepdims=True)

    for copy in row_geom_out + col_geom_out + val_out + wt_out + fwd_out + ret_out:
        copy.wait_send()


def local(
    positions,
    angles,
    areas,
    emissivity,
    emission,
    radiosity_in,
    adjoint_in,
    visibility,
    inlet_patches,
    inlet_weights,
):
    emit_count = lax.axis_size("emit")
    recv_count = lax.axis_size("recv")
    own = areas.shape[0]
    cases = emission.shape[0]
    blocks = own // BLK
    row_total = own * recv_count
    vmem = pl.BlockSpec(memory_space=pltpu.VMEM)
    emit_sem = pltpu.SemaphoreType.DMA((emit_count,))
    recv_sem = pltpu.SemaphoreType.DMA((recv_count,))
    radiosity_out, adjoint_out, grad = pl.pallas_call(
        functools.partial(sweep, emit_count, recv_count),
        out_shape=(
            jax.ShapeDtypeStruct((cases, own), F32),
            jax.ShapeDtypeStruct((cases, own), F32),
            jax.ShapeDtypeStruct((1, own), F32),
        ),
        in_specs=[vmem] * 10,
        out_specs=(vmem, vmem, vmem),
        scratch_shapes=[
            pltpu.VMEM((recv_count, 8, own), F32),
            pltpu.VMEM((emit_count, 8, own), F32),
            pltpu.VMEM((recv_count, cases, own), BF16),
            pltpu.VMEM((emit_count, cases, own), BF16),
            pltpu.VMEM((emit_count * blocks, row_total), F32),
            pltpu.VMEM((recv_count, 48, own), BF16),
            pltpu.VMEM((recv_count, 48, own), BF16),
            pltpu.VMEM((recv_count, 48, own), BF16),
            pltpu.VMEM((emit_count, cases, own), F32),
            pltpu.VMEM((emit_count, cases, own), F32),
            pltpu.VMEM((recv_count, cases, own), F32),
            pltpu.VMEM((recv_count, cases, own), F32),
            recv_sem,
            recv_sem,
            emit_sem,
            emit_sem,
            recv_sem,
            recv_sem,
            emit_sem,
            emit_sem,
            emit_sem,
            emit_sem,
            recv_sem,
            recv_sem,
        ],
        compiler_params=pltpu.CompilerParams(
            collective_id=0, has_side_effects=True, vmem_limit_bytes=40 * 1024 * 1024
        ),
        name="sweep",
    )(
        positions,
        angles,
        areas[None, :],
        emissivity[None, :],
        emission,
        radiosity_in,
        adjoint_in,
        visibility,
        inlet_patches[None, :],
        inlet_weights,
    )
    return (radiosity_out, adjoint_out, grad[0])


def solution(mesh):
    placed = (
        P(None, ("groups", "emit", "recv")),
        P(None, ("groups", "emit", "recv")),
        P(("groups", "emit", "recv")),
        P(("groups", "emit", "recv")),
        P(None, ("groups", "emit", "recv")),
        P(None, ("groups", "emit", "recv")),
        P(None, ("groups", "emit", "recv")),
        P(("groups", "emit"), None),
        P("groups"),
        P(None, "groups"),
    )
    return jax.shard_map(
        local,
        mesh=mesh,
        in_specs=placed,
        out_specs=(
            P(None, ("groups", "emit", "recv")),
            P(None, ("groups", "emit", "recv")),
            P(("groups", "emit", "recv")),
        ),
        check_vma=False,
    )
```

```python
import functools
import math

import jax
import jax.numpy as jnp
from jax import lax
from jax.experimental import pallas as pl
from jax.experimental.pallas import tpu as pltpu
from jax.sharding import PartitionSpec as P

BLK = 128
MESH = pl.DeviceIdType.MESH
F32 = jnp.float32
BF16 = jnp.bfloat16


def flip(index, number):
    bit = 1
    while bit <= number:
        if number & bit:
            index = index + bit * (1 - 2 * ((index // bit) % 2))
        bit *= 2
    return index


def partner(index, number, count):
    if count & (count - 1) == 0:
        return flip(index, number)
    return lax.rem(index + number, count)


def split3(x):
    one = x.astype(BF16).astype(F32)
    rest = x - one
    two = rest.astype(BF16).astype(F32)
    return one, two, rest - two


def row_stack(x):
    one, two, three = split3(x)
    return jnp.concatenate([one, one, two, two, one, three], axis=0)


def col_stack(x):
    one, two, three = split3(x)
    return jnp.concatenate([one, two, one, two, three, one], axis=0)


def dot(a, b, ca, cb):
    return lax.dot_general(a, b, (((ca,), (cb,)), ((), ())), preferred_element_type=F32)


def emitter_forms(geom):
    q, normal, area = geom[0:3], geom[3:6], geom[6:7]
    zero = jnp.zeros_like(area)
    one = jnp.ones_like(area)
    scale = area * (1.0 / math.pi)
    scaled = normal * scale
    offset = -jnp.sum(scaled * q, axis=0, keepdims=True)
    square = jnp.sum(q * q, axis=0, keepdims=True) + area
    cos_emit = jnp.concatenate([scaled, offset, zero, zero, zero, zero], axis=0)
    cos_recv = jnp.concatenate([q, one, zero, zero, zero, zero], axis=0)
    spread = jnp.concatenate([-2.0 * q, square, one, zero, zero, zero], axis=0)
    return cos_emit, cos_recv, spread


def receiver_forms(geom):
    q, normal, area = geom[0:3], geom[3:6], geom[6:7]
    zero = jnp.zeros_like(area)
    one = jnp.ones_like(area)
    offset = -jnp.sum(normal * q, axis=0, keepdims=True)
    square = jnp.sum(q * q, axis=0, keepdims=True)
    cos_emit = jnp.concatenate([q, one, zero, zero, zero, zero], axis=0)
    cos_recv = jnp.concatenate([normal, offset, zero, zero, zero, zero], axis=0)
    spread = jnp.concatenate([q, one, square, zero, zero, zero], axis=0)
    return cos_emit, cos_recv, spread


def sweep(
    emit_count,
    recv_count,
    pos_hbm,
    ang_hbm,
    area_hbm,
    emis_hbm,
    rad_hbm,
    adj_hbm,
    vis_hbm,
    inlet_hbm,
    weight_hbm,
    emission_hbm,
    out_rad,
    out_adj,
    out_grad,
    pos_ref,
    ang_ref,
    area_ref,
    emis_ref,
    rad_ref,
    adj_ref,
    vis_ref,
    inlet_ref,
    weight_ref,
    emission_ref,
    load_sem,
    row_geom,
    col_geom,
    row_val,
    col_wt,
    mask,
    form_a,
    form_b,
    form_s,
    fwd_part,
    fwd_got,
    adj_part,
    adj_got,
    geom_row_send,
    geom_row_recv,
    geom_col_send,
    geom_col_recv,
    val_send,
    val_recv,
    wt_send,
    wt_recv,
    fwd_send,
    fwd_recv,
    ret_send,
    ret_recv,
):
    e = lax.axis_index("emit")
    r = lax.axis_index("recv")
    own = pos_ref.shape[1]
    blocks = own // BLK
    row_total = own * recv_count

    barrier = pltpu.get_barrier_semaphore()
    for k in range(1, recv_count):
        pl.semaphore_signal(
            barrier, inc=1, device_id={"recv": partner(r, k, recv_count)}, device_id_type=MESH
        )
    for k in range(1, emit_count):
        pl.semaphore_signal(
            barrier, inc=1, device_id={"emit": partner(e, k, emit_count)}, device_id_type=MESH
        )

    loads = [
        pltpu.make_async_copy(src, dst, load_sem.at[number])
        for number, (src, dst) in enumerate(
            (
                (pos_hbm, pos_ref),
                (ang_hbm, ang_ref),
                (area_hbm, area_ref),
                (emis_hbm, emis_ref),
                (rad_hbm, rad_ref),
                (adj_hbm, adj_ref),
                (vis_hbm, vis_ref),
                (inlet_hbm, inlet_ref),
                (weight_hbm, weight_ref),
                (emission_hbm, emission_ref),
            )
        )
    ]
    for load in loads:
        load.start()

    for load in loads[:3]:
        load.wait()
    q = pos_ref[...] - 0.5
    angles = ang_ref[...]
    sines = jnp.sin(angles)
    cosines = jnp.cos(angles)
    geometry = jnp.concatenate(
        [
            q,
            sines[0:1] * cosines[1:2],
            sines[0:1] * sines[1:2],
            cosines[0:1],
            area_ref[...],
            jnp.zeros((1, own), F32),
        ],
        axis=0,
    )
    row_geom[r] = geometry
    col_geom[e] = geometry
    pl.semaphore_wait(barrier, recv_count + emit_count - 2)

    def copies(buf, dst, send, recv, axis, me, count, gather):
        out = []
        for k in range(1, count):
            peer = partner(me, k, count)
            out.append(
                pltpu.make_async_remote_copy(
                    src_ref=buf.at[me if gather else peer],
                    dst_ref=dst.at[me],
                    send_sem=send.at[peer],
                    recv_sem=recv.at[me],
                    device_id={axis: peer},
                    device_id_type=MESH,
                )
            )
        return out

    def arrival(dst, send, recv, axis, peer):
        return pltpu.make_async_remote_copy(
            src_ref=dst.at[peer],
            dst_ref=dst.at[peer],
            send_sem=send.at[peer],
            recv_sem=recv.at[peer],
            device_id={axis: peer},
            device_id_type=MESH,
        )

    row_geom_out = copies(row_geom, row_geom, geom_row_send, geom_row_recv, "recv", r, recv_count, True)
    col_geom_out = copies(col_geom, col_geom, geom_col_send, geom_col_recv, "emit", e, emit_count, True)
    for copy in col_geom_out + row_geom_out:
        copy.start()
    for load in loads[3:6]:
        load.wait()
    row_val[r] = rad_ref[...].astype(BF16)
    col_wt[e] = ((1.0 - emis_ref[...]) * adj_ref[...]).astype(BF16)
    val_out = copies(row_val, row_val, val_send, val_recv, "recv", r, recv_count, True)
    wt_out = copies(col_wt, col_wt, wt_send, wt_recv, "emit", e, emit_count, True)
    for copy in wt_out + val_out:
        copy.start()

    loads[6].wait()
    all_blocks = vis_ref.shape[1]
    col_blocks = emit_count * blocks
    number = lax.broadcasted_iota(jnp.int32, (col_blocks, all_blocks), 0)
    wanted = (lax.div(number, blocks) * recv_count + r) * blocks + lax.rem(number, blocks)
    chosen = (lax.broadcasted_iota(jnp.int32, (col_blocks, all_blocks), 1) == wanted).astype(F32)
    tile_mask = dot(chosen.astype(BF16), vis_ref[...].astype(F32).astype(BF16), 1, 1)
    row_blocks = recv_count * blocks
    spot = lax.broadcasted_iota(jnp.int32, (row_blocks, row_total), 1) // BLK
    expand = (lax.broadcasted_iota(jnp.int32, (row_blocks, row_total), 0) == spot).astype(F32)
    mask[...] = dot(tile_mask.astype(BF16), expand.astype(BF16), 1, 0)

    for k in range(recv_count):
        peer = partner(r, k, recv_count)
        if k:
            arrival(row_geom, geom_row_send, geom_row_recv, "recv", peer).wait_recv()
        for form, buf in zip(emitter_forms(row_geom[peer]), (form_a, form_b, form_s)):
            buf[peer] = row_stack(form).astype(BF16)

    for k in range(recv_count):
        adj_part[k] = jnp.zeros(adj_part.shape[1:], F32)

    lane = lax.broadcasted_iota(jnp.int32, (1, own), 1) // BLK

    def columns(peer):
        forms = [col_stack(form) for form in receiver_forms(col_geom[peer])]
        spaced = jnp.concatenate([jnp.where(lane == b, forms[0], 0.0) for b in range(blocks)], axis=0)
        side_a = spaced.T.astype(BF16)
        side_b = forms[1].T.astype(BF16)
        side_s = forms[2].T.astype(BF16)
        weight = col_wt[peer]

        def rows(number, total):
            start = pl.multiple_of(number * own, own)
            base = form_a[number]
            masked = jnp.concatenate(
                [
                    base * mask[pl.ds(peer * blocks + b, 1), pl.ds(start, own)].astype(BF16)
                    for b in range(blocks)
                ],
                axis=0,
            )
            cos_emit = jnp.maximum(dot(side_a, masked, 1, 0), 0.0)
            cos_recv = jnp.maximum(dot(side_b, form_b[number], 1, 0), 0.0)
            spread = dot(side_s, form_s[number], 1, 0)
            tile = (cos_emit * cos_recv * pl.reciprocal(spread * spread, approx=True)).astype(BF16)
            adj_part[number] += dot(weight, tile, 1, 0)
            return total + dot(row_val[number], tile, 1, 1)

        zero = jnp.zeros(fwd_part.shape[1:], F32)
        fwd_part[peer] = lax.fori_loop(0, recv_count, rows, zero, unroll=recv_count <= 4)

    for k in range(1, recv_count):
        arrival(row_val, val_send, val_recv, "recv", partner(r, k, recv_count)).wait_recv()

    fwd_out = copies(fwd_part, fwd_got, fwd_send, fwd_recv, "emit", e, emit_count, False)
    columns(e)
    for k in reversed(range(1, emit_count)):
        peer = partner(e, k, emit_count)
        arrival(col_geom, geom_col_send, geom_col_recv, "emit", peer).wait_recv()
        arrival(col_wt, wt_send, wt_recv, "emit", peer).wait_recv()
        columns(peer)
        fwd_out[k - 1].start()

    ret_out = copies(adj_part, adj_got, ret_send, ret_recv, "recv", r, recv_count, False)
    for copy in ret_out:
        copy.start()

    for load in loads[7:]:
        load.wait()
    patch = (e * recv_count + r) * own + lax.broadcasted_iota(jnp.int32, (own, 1), 0)
    selector = jnp.where(inlet_ref[...] == patch, 1.0, 0.0).astype(BF16)
    weights = weight_ref[...]
    high = weights.astype(BF16)
    low = (weights - high.astype(F32)).astype(BF16)
    source = dot(high, selector, 1, 1) + dot(low, selector, 1, 1)

    incoming = fwd_part[e]
    for k in range(1, emit_count):
        peer = partner(e, k, emit_count)
        arrival(fwd_got, fwd_send, fwd_recv, "emit", peer).wait_recv()
        incoming = incoming + fwd_got[peer]
    emission = emission_ref[...]
    share = emis_ref[...]
    out_rad[...] = share * emission + (1.0 - share) * incoming
    returned = adj_part[r]
    for k in range(1, recv_count):
        peer = partner(r, k, recv_count)
        arrival(adj_got, ret_send, ret_recv, "recv", peer).wait_recv()
        returned = returned + adj_got[peer]
    adjoint = source + returned
    out_adj[...] = adjoint
    out_grad[...] = jnp.sum(adjoint * (emission - incoming), axis=0, keepdims=True)

    for copy in row_geom_out + col_geom_out + val_out + wt_out + fwd_out + ret_out:
        copy.wait_send()


def finish(rad_ref, adj_ref, grad_ref, rad_hbm, adj_hbm, grad_hbm, sem):
    stores = [
        pltpu.make_async_copy(rad_ref, rad_hbm, sem.at[0]),
        pltpu.make_async_copy(adj_ref, adj_hbm, sem.at[1]),
        pltpu.make_async_copy(grad_ref, grad_hbm, sem.at[2]),
    ]
    for copy in stores:
        copy.start()
    for copy in stores:
        copy.wait()


def local(
    positions,
    angles,
    areas,
    emissivity,
    emission,
    radiosity_in,
    adjoint_in,
    visibility,
    inlet_patches,
    inlet_weights,
):
    emit_count = lax.axis_size("emit")
    recv_count = lax.axis_size("recv")
    own = areas.shape[0]
    cases = emission.shape[0]
    blocks = own // BLK
    row_total = own * recv_count
    vmem = pl.BlockSpec(memory_space=pltpu.VMEM)
    hbm = pl.BlockSpec(memory_space=pltpu.HBM)
    emit_sem = pltpu.SemaphoreType.DMA((emit_count,))
    recv_sem = pltpu.SemaphoreType.DMA((recv_count,))
    operands = (
        positions,
        angles,
        areas[None, :],
        emissivity[None, :],
        radiosity_in,
        adjoint_in,
        visibility,
        inlet_patches[None, :],
        inlet_weights,
        emission,
    )
    flat = jax.ShapeDtypeStruct((cases, own), F32)
    results = (flat, flat, jax.ShapeDtypeStruct((1, own), F32))
    swept = pl.pallas_call(
        functools.partial(sweep, emit_count, recv_count),
        out_shape=results,
        in_specs=[hbm] * len(operands),
        out_specs=(vmem, vmem, vmem),
        scratch_shapes=[pltpu.VMEM(x.shape, x.dtype) for x in operands]
        + [
            pltpu.SemaphoreType.DMA((len(operands),)),
            pltpu.VMEM((recv_count, 8, own), F32),
            pltpu.VMEM((emit_count, 8, own), F32),
            pltpu.VMEM((recv_count, cases, own), BF16),
            pltpu.VMEM((emit_count, cases, own), BF16),
            pltpu.VMEM((emit_count * blocks, row_total), F32),
            pltpu.VMEM((recv_count, 48, own), BF16),
            pltpu.VMEM((recv_count, 48, own), BF16),
            pltpu.VMEM((recv_count, 48, own), BF16),
            pltpu.VMEM((emit_count, cases, own), F32),
            pltpu.VMEM((emit_count, cases, own), F32),
            pltpu.VMEM((recv_count, cases, own), F32),
            pltpu.VMEM((recv_count, cases, own), F32),
            recv_sem,
            recv_sem,
            emit_sem,
            emit_sem,
            recv_sem,
            recv_sem,
            emit_sem,
            emit_sem,
            emit_sem,
            emit_sem,
            recv_sem,
            recv_sem,
        ],
        compiler_params=pltpu.CompilerParams(
            collective_id=0, has_side_effects=True, vmem_limit_bytes=40 * 1024 * 1024
        ),
        name="sweep",
    )(*operands)
    radiosity_out, adjoint_out, grad = pl.pallas_call(
        finish,
        out_shape=results,
        in_specs=[vmem, vmem, vmem],
        out_specs=(hbm, hbm, hbm),
        scratch_shapes=[pltpu.SemaphoreType.DMA((3,))],
        name="finish",
    )(*swept)
    return (radiosity_out, adjoint_out, grad[0])


def solution(mesh):
    placed = (
        P(None, ("groups", "emit", "recv")),
        P(None, ("groups", "emit", "recv")),
        P(("groups", "emit", "recv")),
        P(("groups", "emit", "recv")),
        P(None, ("groups", "emit", "recv")),
        P(None, ("groups", "emit", "recv")),
        P(None, ("groups", "emit", "recv")),
        P(("groups", "emit"), None),
        P("groups"),
        P(None, "groups"),
    )
    return jax.shard_map(
        local,
        mesh=mesh,
        in_specs=placed,
        out_specs=(
            P(None, ("groups", "emit", "recv")),
            P(None, ("groups", "emit", "recv")),
            P(("groups", "emit", "recv")),
        ),
        check_vma=False,
    )
```

```python
import functools
import math

import jax
import jax.numpy as jnp
from jax import lax
from jax.experimental import pallas as pl
from jax.experimental.pallas import tpu as pltpu
from jax.sharding import PartitionSpec as P

BLK = 128
MESH = pl.DeviceIdType.MESH
F32 = jnp.float32
BF16 = jnp.bfloat16


def flip(index, number):
    bit = 1
    while bit <= number:
        if number & bit:
            index = index + bit * (1 - 2 * ((index // bit) % 2))
        bit *= 2
    return index


def partner(index, number, count):
    if count & (count - 1) == 0:
        return flip(index, number)
    return lax.rem(index + number, count)


def split3(x):
    one = x.astype(BF16).astype(F32)
    rest = x - one
    two = rest.astype(BF16).astype(F32)
    return one, two, rest - two


def row_stack(x):
    one, two, three = split3(x)
    return jnp.concatenate([one, one, two, two, one, three], axis=0)


def col_stack(x):
    one, two, three = split3(x)
    return jnp.concatenate([one, two, one, two, three, one], axis=0)


def dot(a, b, ca, cb):
    return lax.dot_general(a, b, (((ca,), (cb,)), ((), ())), preferred_element_type=F32)


def emitter_forms(geom):
    q, normal, area = geom[0:3], geom[3:6], geom[6:7]
    zero = jnp.zeros_like(area)
    one = jnp.ones_like(area)
    scale = area * (1.0 / math.pi)
    scaled = normal * scale
    offset = -jnp.sum(scaled * q, axis=0, keepdims=True)
    square = jnp.sum(q * q, axis=0, keepdims=True) + area
    cos_emit = jnp.concatenate([scaled, offset, zero, zero, zero, zero], axis=0)
    cos_recv = jnp.concatenate([q, one, zero, zero, zero, zero], axis=0)
    spread = jnp.concatenate([-2.0 * q, square, one, zero, zero, zero], axis=0)
    return cos_emit, cos_recv, spread


def receiver_forms(geom):
    q, normal, area = geom[0:3], geom[3:6], geom[6:7]
    zero = jnp.zeros_like(area)
    one = jnp.ones_like(area)
    offset = -jnp.sum(normal * q, axis=0, keepdims=True)
    square = jnp.sum(q * q, axis=0, keepdims=True)
    cos_emit = jnp.concatenate([q, one, zero, zero, zero, zero], axis=0)
    cos_recv = jnp.concatenate([normal, offset, zero, zero, zero, zero], axis=0)
    spread = jnp.concatenate([q, one, square, zero, zero, zero], axis=0)
    return cos_emit, cos_recv, spread


def sweep(
    emit_count,
    recv_count,
    pos_hbm,
    ang_hbm,
    area_hbm,
    emis_hbm,
    rad_hbm,
    adj_hbm,
    vis_hbm,
    inlet_hbm,
    weight_hbm,
    emission_hbm,
    own_hbm,
    lit_hbm,
    diff_hbm,
    src_hbm,
    ret_hbm,
    pos_ref,
    ang_ref,
    area_ref,
    emis_ref,
    rad_ref,
    adj_ref,
    vis_ref,
    inlet_ref,
    weight_ref,
    emission_ref,
    out_own,
    out_lit,
    out_diff,
    out_src,
    out_ret,
    load_sem,
    store_sem,
    row_geom,
    col_geom,
    row_val,
    col_wt,
    mask,
    form_a,
    form_b,
    form_s,
    fwd_part,
    fwd_got,
    adj_part,
    adj_got,
    geom_row_send,
    geom_row_recv,
    geom_col_send,
    geom_col_recv,
    val_send,
    val_recv,
    wt_send,
    wt_recv,
    fwd_send,
    fwd_recv,
    ret_send,
    ret_recv,
):
    e = lax.axis_index("emit")
    r = lax.axis_index("recv")
    own = pos_ref.shape[1]
    blocks = own // BLK
    row_total = own * recv_count

    barrier = pltpu.get_barrier_semaphore()
    for k in range(1, recv_count):
        pl.semaphore_signal(
            barrier, inc=1, device_id={"recv": partner(r, k, recv_count)}, device_id_type=MESH
        )
    for k in range(1, emit_count):
        pl.semaphore_signal(
            barrier, inc=1, device_id={"emit": partner(e, k, emit_count)}, device_id_type=MESH
        )

    loads = [
        pltpu.make_async_copy(src, dst, load_sem.at[number])
        for number, (src, dst) in enumerate(
            (
                (pos_hbm, pos_ref),
                (ang_hbm, ang_ref),
                (area_hbm, area_ref),
                (emis_hbm, emis_ref),
                (rad_hbm, rad_ref),
                (adj_hbm, adj_ref),
                (vis_hbm, vis_ref),
                (inlet_hbm, inlet_ref),
                (weight_hbm, weight_ref),
                (emission_hbm, emission_ref),
            )
        )
    ]
    stores = [
        pltpu.make_async_copy(src, dst, store_sem.at[number])
        for number, (src, dst) in enumerate(
            (
                (out_own, own_hbm),
                (out_src, src_hbm),
                (out_lit, lit_hbm),
                (out_diff, diff_hbm),
                (out_ret, ret_hbm),
            )
        )
    ]
    for load in loads:
        load.start()

    for load in loads[:3]:
        load.wait()
    q = pos_ref[...] - 0.5
    angles = ang_ref[...]
    sines = jnp.sin(angles)
    cosines = jnp.cos(angles)
    geometry = jnp.concatenate(
        [
            q,
            sines[0:1] * cosines[1:2],
            sines[0:1] * sines[1:2],
            cosines[0:1],
            area_ref[...],
            jnp.zeros((1, own), F32),
        ],
        axis=0,
    )
    row_geom[r] = geometry
    col_geom[e] = geometry
    pl.semaphore_wait(barrier, recv_count + emit_count - 2)

    def copies(buf, dst, send, recv, axis, me, count, gather):
        out = []
        for k in range(1, count):
            peer = partner(me, k, count)
            out.append(
                pltpu.make_async_remote_copy(
                    src_ref=buf.at[me if gather else peer],
                    dst_ref=dst.at[me],
                    send_sem=send.at[peer],
                    recv_sem=recv.at[me],
                    device_id={axis: peer},
                    device_id_type=MESH,
                )
            )
        return out

    def arrival(dst, send, recv, axis, peer):
        return pltpu.make_async_remote_copy(
            src_ref=dst.at[peer],
            dst_ref=dst.at[peer],
            send_sem=send.at[peer],
            recv_sem=recv.at[peer],
            device_id={axis: peer},
            device_id_type=MESH,
        )

    row_geom_out = copies(row_geom, row_geom, geom_row_send, geom_row_recv, "recv", r, recv_count, True)
    col_geom_out = copies(col_geom, col_geom, geom_col_send, geom_col_recv, "emit", e, emit_count, True)
    for copy in col_geom_out + row_geom_out:
        copy.start()
    for load in loads[3:6]:
        load.wait()
    row_val[r] = rad_ref[...].astype(BF16)
    col_wt[e] = ((1.0 - emis_ref[...]) * adj_ref[...]).astype(BF16)
    val_out = copies(row_val, row_val, val_send, val_recv, "recv", r, recv_count, True)
    wt_out = copies(col_wt, col_wt, wt_send, wt_recv, "emit", e, emit_count, True)
    for copy in wt_out + val_out:
        copy.start()

    loads[6].wait()
    all_blocks = vis_ref.shape[1]
    col_blocks = emit_count * blocks
    number = lax.broadcasted_iota(jnp.int32, (col_blocks, all_blocks), 0)
    wanted = (lax.div(number, blocks) * recv_count + r) * blocks + lax.rem(number, blocks)
    chosen = (lax.broadcasted_iota(jnp.int32, (col_blocks, all_blocks), 1) == wanted).astype(F32)
    tile_mask = dot(chosen.astype(BF16), vis_ref[...].astype(F32).astype(BF16), 1, 1)
    row_blocks = recv_count * blocks
    spot = lax.broadcasted_iota(jnp.int32, (row_blocks, row_total), 1) // BLK
    expand = (lax.broadcasted_iota(jnp.int32, (row_blocks, row_total), 0) == spot).astype(F32)
    mask[...] = dot(tile_mask.astype(BF16), expand.astype(BF16), 1, 0)

    for k in range(recv_count):
        peer = partner(r, k, recv_count)
        if k:
            arrival(row_geom, geom_row_send, geom_row_recv, "recv", peer).wait_recv()
        for form, buf in zip(emitter_forms(row_geom[peer]), (form_a, form_b, form_s)):
            buf[peer] = row_stack(form).astype(BF16)

    for k in range(recv_count):
        adj_part[k] = jnp.zeros(adj_part.shape[1:], F32)

    lane = lax.broadcasted_iota(jnp.int32, (1, own), 1) // BLK

    def columns(peer):
        forms = [col_stack(form) for form in receiver_forms(col_geom[peer])]
        spaced = jnp.concatenate([jnp.where(lane == b, forms[0], 0.0) for b in range(blocks)], axis=0)
        side_a = spaced.T.astype(BF16)
        side_b = forms[1].T.astype(BF16)
        side_s = forms[2].T.astype(BF16)
        weight = col_wt[peer]

        def rows(number, total):
            start = pl.multiple_of(number * own, own)
            base = form_a[number]
            masked = jnp.concatenate(
                [
                    base * mask[pl.ds(peer * blocks + b, 1), pl.ds(start, own)].astype(BF16)
                    for b in range(blocks)
                ],
                axis=0,
            )
            cos_emit = jnp.maximum(dot(side_a, masked, 1, 0), 0.0)
            cos_recv = jnp.maximum(dot(side_b, form_b[number], 1, 0), 0.0)
            spread = dot(side_s, form_s[number], 1, 0)
            tile = (cos_emit * cos_recv * pl.reciprocal(spread * spread, approx=True)).astype(BF16)
            adj_part[number] += dot(weight, tile, 1, 0)
            return total + dot(row_val[number], tile, 1, 1)

        zero = jnp.zeros(fwd_part.shape[1:], F32)
        fwd_part[peer] = lax.fori_loop(0, recv_count, rows, zero, unroll=recv_count <= 4)

    for k in range(1, recv_count):
        arrival(row_val, val_send, val_recv, "recv", partner(r, k, recv_count)).wait_recv()

    fwd_out = copies(fwd_part, fwd_got, fwd_send, fwd_recv, "emit", e, emit_count, False)
    columns(e)
    for k in reversed(range(1, emit_count)):
        peer = partner(e, k, emit_count)
        arrival(col_geom, geom_col_send, geom_col_recv, "emit", peer).wait_recv()
        arrival(col_wt, wt_send, wt_recv, "emit", peer).wait_recv()
        columns(peer)
        fwd_out[k - 1].start()

    ret_out = copies(adj_part, adj_got, ret_send, ret_recv, "recv", r, recv_count, False)
    for copy in ret_out:
        copy.start()

    for load in loads[7:]:
        load.wait()
    patch = (e * recv_count + r) * own + lax.broadcasted_iota(jnp.int32, (own, 1), 0)
    selector = jnp.where(inlet_ref[...] == patch, 1.0, 0.0).astype(BF16)
    weights = weight_ref[...]
    high = weights.astype(BF16)
    low = (weights - high.astype(F32)).astype(BF16)
    out_src[...] = dot(high, selector, 1, 1) + dot(low, selector, 1, 1)

    stores[1].start()
    share = emis_ref[...]
    emission = emission_ref[...]
    out_own[...] = share * emission
    stores[0].start()

    incoming = fwd_part[e]
    for k in range(1, emit_count):
        peer = partner(e, k, emit_count)
        arrival(fwd_got, fwd_send, fwd_recv, "emit", peer).wait_recv()
        incoming = incoming + fwd_got[peer]
    out_lit[...] = (1.0 - share) * incoming
    stores[2].start()
    out_diff[...] = emission - incoming
    stores[3].start()
    returned = adj_part[r]
    for k in range(1, recv_count):
        peer = partner(r, k, recv_count)
        arrival(adj_got, ret_send, ret_recv, "recv", peer).wait_recv()
        returned = returned + adj_got[peer]
    out_ret[...] = returned
    stores[4].start()

    for copy in row_geom_out + col_geom_out + val_out + wt_out + fwd_out + ret_out:
        copy.wait_send()
    for copy in stores:
        copy.wait()


def local(
    positions,
    angles,
    areas,
    emissivity,
    emission,
    radiosity_in,
    adjoint_in,
    visibility,
    inlet_patches,
    inlet_weights,
):
    emit_count = lax.axis_size("emit")
    recv_count = lax.axis_size("recv")
    own = areas.shape[0]
    cases = emission.shape[0]
    blocks = own // BLK
    row_total = own * recv_count
    hbm = pl.BlockSpec(memory_space=pltpu.HBM)
    emit_sem = pltpu.SemaphoreType.DMA((emit_count,))
    recv_sem = pltpu.SemaphoreType.DMA((recv_count,))
    operands = (
        positions,
        angles,
        areas[None, :],
        emissivity[None, :],
        radiosity_in,
        adjoint_in,
        visibility,
        inlet_patches[None, :],
        inlet_weights,
        emission,
    )
    flat = jax.ShapeDtypeStruct((cases, own), F32)
    emitted, lit, difference, source, returned = pl.pallas_call(
        functools.partial(sweep, emit_count, recv_count),
        out_shape=(flat,) * 5,
        in_specs=[hbm] * len(operands),
        out_specs=(hbm,) * 5,
        scratch_shapes=[pltpu.VMEM(x.shape, x.dtype) for x in operands]
        + [pltpu.VMEM((cases, own), F32)] * 5
        + [
            pltpu.SemaphoreType.DMA((len(operands),)),
            pltpu.SemaphoreType.DMA((5,)),
            pltpu.VMEM((recv_count, 8, own), F32),
            pltpu.VMEM((emit_count, 8, own), F32),
            pltpu.VMEM((recv_count, cases, own), BF16),
            pltpu.VMEM((emit_count, cases, own), BF16),
            pltpu.VMEM((emit_count * blocks, row_total), F32),
            pltpu.VMEM((recv_count, 48, own), BF16),
            pltpu.VMEM((recv_count, 48, own), BF16),
            pltpu.VMEM((recv_count, 48, own), BF16),
            pltpu.VMEM((emit_count, cases, own), F32),
            pltpu.VMEM((emit_count, cases, own), F32),
            pltpu.VMEM((recv_count, cases, own), F32),
            pltpu.VMEM((recv_count, cases, own), F32),
            recv_sem,
            recv_sem,
            emit_sem,
            emit_sem,
            recv_sem,
            recv_sem,
            emit_sem,
            emit_sem,
            emit_sem,
            emit_sem,
            recv_sem,
            recv_sem,
        ],
        compiler_params=pltpu.CompilerParams(
            collective_id=0, has_side_effects=True, vmem_limit_bytes=64 * 1024 * 1024
        ),
        name="sweep",
    )(*operands)
    radiosity_out = emitted + lit
    adjoint_out = source + returned
    grad = jnp.sum(adjoint_out * difference, axis=0)
    return (radiosity_out, adjoint_out, grad)


def solution(mesh):
    placed = (
        P(None, ("groups", "emit", "recv")),
        P(None, ("groups", "emit", "recv")),
        P(("groups", "emit", "recv")),
        P(("groups", "emit", "recv")),
        P(None, ("groups", "emit", "recv")),
        P(None, ("groups", "emit", "recv")),
        P(None, ("groups", "emit", "recv")),
        P(("groups", "emit"), None),
        P("groups"),
        P(None, "groups"),
    )
    return jax.shard_map(
        local,
        mesh=mesh,
        in_specs=placed,
        out_specs=(
            P(None, ("groups", "emit", "recv")),
            P(None, ("groups", "emit", "recv")),
            P(("groups", "emit", "recv")),
        ),
        check_vma=False,
    )
```

```python
import functools
import math

import jax
import jax.numpy as jnp
from jax import lax
from jax.experimental import pallas as pl
from jax.experimental.pallas import tpu as pltpu
from jax.sharding import PartitionSpec as P

BLK = 128
MESH = pl.DeviceIdType.MESH
F32 = jnp.float32
BF16 = jnp.bfloat16


def flip(index, number):
    bit = 1
    while bit <= number:
        if number & bit:
            index = index + bit * (1 - 2 * ((index // bit) % 2))
        bit *= 2
    return index


def partner(index, number, count):
    if count & (count - 1) == 0:
        return flip(index, number)
    return lax.rem(index + number, count)


def split3(x):
    one = x.astype(BF16).astype(F32)
    rest = x - one
    two = rest.astype(BF16).astype(F32)
    return one, two, rest - two


def dot(a, b, ca, cb):
    return lax.dot_general(a, b, (((ca,), (cb,)), ((), ())), preferred_element_type=F32)


def sine_cosine(angles):
    half = 0.5 * angles
    square = half * half
    sine = jnp.full_like(half, 1.0 / math.factorial(13))
    cosine = jnp.full_like(half, 1.0 / math.factorial(14))
    cosine = cosine * square - 1.0 / math.factorial(12)
    for order in (11, 9, 7, 5, 3, 1):
        sign = -1.0 if order % 4 == 3 else 1.0
        sine = sine * square + sign / math.factorial(order)
        cosine = cosine * square - sign / math.factorial(order - 1)
    sine = sine * half
    cosine = -cosine
    return 2.0 * sine * cosine, 1.0 - 2.0 * sine * sine


def own_blocks_of(q, angles, area):
    sines, cosines = sine_cosine(angles)
    normal = jnp.concatenate(
        [sines[0:1] * cosines[1:2], sines[0:1] * sines[1:2], cosines[0:1]], axis=0
    )
    offset = -jnp.sum(normal * q, axis=0, keepdims=True)
    square = jnp.sum(q * q, axis=0, keepdims=True)
    scale = area * (1.0 / math.pi)
    emitter = jnp.concatenate([normal * scale, offset * scale, q, square + area], axis=0)
    receiver = jnp.concatenate([normal, offset, q, square], axis=0)
    return emitter, receiver


def emitter_forms(block):
    parts = split3(block)
    row = lax.broadcasted_iota(jnp.int32, block.shape, 0)
    order = (0, 0, 1, 1, 0, 2)
    stacks = []
    for place in (None, 7, 3):
        form = parts
        if place is not None:
            form = [jnp.where(row == place, float(n == 0), part) for n, part in enumerate(parts)]
        stacks.append(jnp.concatenate([form[n] for n in order], axis=0))
    return stacks


def receiver_forms(block):
    row = lax.broadcasted_iota(jnp.int32, block.shape, 0)
    turned = jnp.concatenate([block[4:8], block[0:4]], axis=0)
    cos_emit, cos_recv, spread = [], [], []
    for n, (part, swapped) in enumerate(zip(split3(block), split3(turned))):
        one = float(n == 0)
        cos_emit.append(jnp.where(row < 3, swapped, jnp.where(row == 3, one, 0.0)))
        cos_recv.append(jnp.where(row >= 4, swapped, 0.0))
        inner = jnp.where(row == 7, one, -2.0 * part)
        spread.append(jnp.where(row == 3, swapped, jnp.where(row >= 4, inner, 0.0)))
    order = (0, 1, 0, 1, 2, 0)
    return [
        jnp.concatenate([form[n] for n in order], axis=0) for form in (cos_emit, cos_recv, spread)
    ]


def sweep(
    emit_count,
    recv_count,
    pos_hbm,
    ang_hbm,
    area_hbm,
    emis_hbm,
    rad_hbm,
    adj_hbm,
    vis_hbm,
    inlet_hbm,
    weight_hbm,
    emission_hbm,
    rad_out_hbm,
    adj_out_hbm,
    grad_out_hbm,
    pos_ref,
    ang_ref,
    area_ref,
    emis_ref,
    rad_ref,
    adj_ref,
    vis_ref,
    inlet_ref,
    weight_ref,
    emission_ref,
    out_rad,
    out_adj,
    out_grad,
    load_sem,
    store_sem,
    row_geom,
    col_geom,
    row_val,
    col_wt,
    mask,
    form_a,
    form_b,
    form_s,
    tile,
    value_t,
    fwd_part,
    fwd_got,
    adj_part,
    adj_got,
    geom_row_send,
    geom_row_recv,
    geom_col_send,
    geom_col_recv,
    val_send,
    val_recv,
    wt_send,
    wt_recv,
    fwd_send,
    fwd_recv,
    ret_send,
    ret_recv,
):
    e = lax.axis_index("emit")
    r = lax.axis_index("recv")
    own = pos_ref.shape[1]
    blocks = own // BLK
    row_total = own * recv_count

    barrier = pltpu.get_barrier_semaphore()
    for k in range(1, recv_count):
        pl.semaphore_signal(
            barrier, inc=1, device_id={"recv": partner(r, k, recv_count)}, device_id_type=MESH
        )
    for k in range(1, emit_count):
        pl.semaphore_signal(
            barrier, inc=1, device_id={"emit": partner(e, k, emit_count)}, device_id_type=MESH
        )

    loads = [
        pltpu.make_async_copy(src, dst, load_sem.at[number])
        for number, (src, dst) in enumerate(
            (
                (pos_hbm, pos_ref),
                (ang_hbm, ang_ref),
                (area_hbm, area_ref),
                (emis_hbm, emis_ref),
                (rad_hbm, rad_ref),
                (adj_hbm, adj_ref),
                (vis_hbm, vis_ref),
                (inlet_hbm, inlet_ref),
                (weight_hbm, weight_ref),
                (emission_hbm, emission_ref),
            )
        )
    ]
    stores = [
        pltpu.make_async_copy(src, dst, store_sem.at[number])
        for number, (src, dst) in enumerate(
            (
                (out_rad, rad_out_hbm),
                (out_adj, adj_out_hbm),
                (out_grad, grad_out_hbm),
            )
        )
    ]
    for load in loads:
        load.start()

    for load in loads[:3]:
        load.wait()
    emitter, receiver = own_blocks_of(pos_ref[...] - 0.5, ang_ref[...], area_ref[...])
    row_geom[r] = emitter
    col_geom[e] = receiver

    pl.semaphore_wait(barrier, recv_count + emit_count - 2)

    def copies(buf, dst, send, recv, axis, me, count, gather):
        out = []
        for k in range(1, count):
            peer = partner(me, k, count)
            out.append(
                pltpu.make_async_remote_copy(
                    src_ref=buf.at[me if gather else peer],
                    dst_ref=dst.at[me],
                    send_sem=send.at[peer],
                    recv_sem=recv.at[me],
                    device_id={axis: peer},
                    device_id_type=MESH,
                )
            )
        return out

    def arrival(dst, send, recv, axis, peer):
        return pltpu.make_async_remote_copy(
            src_ref=dst.at[peer],
            dst_ref=dst.at[peer],
            send_sem=send.at[peer],
            recv_sem=recv.at[peer],
            device_id={axis: peer},
            device_id_type=MESH,
        )

    row_geom_out = copies(row_geom, row_geom, geom_row_send, geom_row_recv, "recv", r, recv_count, True)
    col_geom_out = copies(col_geom, col_geom, geom_col_send, geom_col_recv, "emit", e, emit_count, True)
    for copy in col_geom_out + row_geom_out:
        copy.start()
    for load in loads[3:6]:
        load.wait()
    row_val[r] = rad_ref[...].astype(BF16)
    col_wt[e] = ((1.0 - emis_ref[...]) * adj_ref[...]).astype(BF16)
    val_out = copies(row_val, row_val, val_send, val_recv, "recv", r, recv_count, True)
    wt_out = copies(col_wt, col_wt, wt_send, wt_recv, "emit", e, emit_count, True)
    for copy in wt_out + val_out:
        copy.start()

    loads[6].wait()
    all_blocks = vis_ref.shape[1]
    col_blocks = emit_count * blocks
    number = lax.broadcasted_iota(jnp.int32, (col_blocks, all_blocks), 0)
    wanted = (lax.div(number, blocks) * recv_count + r) * blocks + lax.rem(number, blocks)
    chosen = (lax.broadcasted_iota(jnp.int32, (col_blocks, all_blocks), 1) == wanted).astype(F32)
    tile_mask = dot(chosen.astype(BF16), vis_ref[...].astype(F32).astype(BF16), 1, 1)
    row_blocks = recv_count * blocks
    spot = lax.broadcasted_iota(jnp.int32, (row_blocks, row_total), 1) // BLK
    expand = (lax.broadcasted_iota(jnp.int32, (row_blocks, row_total), 0) == spot).astype(F32)
    mask[...] = dot(tile_mask.astype(BF16), expand.astype(BF16), 1, 0)

    for k in range(recv_count):
        peer = partner(r, k, recv_count)
        if k:
            arrival(row_geom, geom_row_send, geom_row_recv, "recv", peer).wait_recv()
        for form, buf in zip(emitter_forms(row_geom[peer]), (form_a, form_b, form_s)):
            buf[peer] = form.astype(BF16)

    lane = lax.broadcasted_iota(jnp.int32, (1, own), 1) // BLK
    group = tile.shape[1] // own

    def columns(peer, first):
        forms = receiver_forms(col_geom[peer])
        spaced = jnp.concatenate([jnp.where(lane == b, forms[0], 0.0) for b in range(blocks)], axis=0)
        side_a = spaced.astype(BF16).T
        side_b = forms[1].astype(BF16).T
        side_s = forms[2].astype(BF16).T
        weight = col_wt[peer]

        def rows(chunk, total):
            for inner in range(group):
                number = chunk * group + inner
                start = pl.multiple_of(number * own, own)
                base = form_a[number]
                masked = jnp.concatenate(
                    [
                        base * mask[pl.ds(peer * blocks + b, 1), pl.ds(start, own)].astype(BF16)
                        for b in range(blocks)
                    ],
                    axis=0,
                )
                cos_emit = jnp.maximum(dot(side_a, masked, 1, 0), 0.0)
                cos_recv = jnp.maximum(dot(side_b, form_b[number], 1, 0), 0.0)
                spread = dot(side_s, form_s[number], 1, 0)
                tile[:, inner * own : (inner + 1) * own] = (
                    cos_emit * cos_recv * pl.reciprocal(spread * spread, approx=True)
                ).astype(BF16)
            whole = tile[...]
            back = dot(weight, whole, 1, 0)
            for inner in range(group):
                number = chunk * group + inner
                piece = back[:, inner * own : (inner + 1) * own]
                adj_part[number] = piece if first else adj_part[number] + piece
            width = group * own
            value = value_t[pl.ds(pl.multiple_of(chunk * width, width), width), :]
            return total + dot(whole, value, 1, 0)

        total = jnp.zeros((own, value_t.shape[1]), F32)
        if recv_count == group:
            total = rows(0, total)
        else:
            total = lax.fori_loop(0, recv_count // group, rows, total)
        fwd_part[peer] = total.T

    for k in range(1, recv_count):
        arrival(row_val, val_send, val_recv, "recv", partner(r, k, recv_count)).wait_recv()
    for k in range(recv_count):
        value_t[k * own : (k + 1) * own, :] = row_val[k].T

    fwd_out = copies(fwd_part, fwd_got, fwd_send, fwd_recv, "emit", e, emit_count, False)
    columns(e, True)
    for k in reversed(range(1, emit_count)):
        peer = partner(e, k, emit_count)
        arrival(col_geom, geom_col_send, geom_col_recv, "emit", peer).wait_recv()
        arrival(col_wt, wt_send, wt_recv, "emit", peer).wait_recv()
        columns(peer, False)
        fwd_out[k - 1].start()

    ret_out = copies(adj_part, adj_got, ret_send, ret_recv, "recv", r, recv_count, False)
    for copy in ret_out:
        copy.start()

    for load in loads[7:]:
        load.wait()
    patch = (e * recv_count + r) * own + lax.broadcasted_iota(jnp.int32, (own, 1), 0)
    selector = jnp.where(inlet_ref[...] == patch, 1.0, 0.0).astype(BF16)
    weights = weight_ref[...]
    high = weights.astype(BF16)
    low = (weights - high.astype(F32)).astype(BF16)
    source = dot(high, selector, 1, 1) + dot(low, selector, 1, 1)

    share = emis_ref[...]
    emission = emission_ref[...]

    incoming = fwd_part[e]
    for k in range(1, emit_count):
        peer = partner(e, k, emit_count)
        arrival(fwd_got, fwd_send, fwd_recv, "emit", peer).wait_recv()
        incoming = incoming + fwd_got[peer]
    out_rad[...] = share * emission + (1.0 - share) * incoming
    stores[0].start()
    returned = adj_part[r]
    for k in range(1, recv_count):
        peer = partner(r, k, recv_count)
        arrival(adj_got, ret_send, ret_recv, "recv", peer).wait_recv()
        returned = returned + adj_got[peer]
    adjoint = source + returned
    out_adj[...] = adjoint
    stores[1].start()
    out_grad[...] = jnp.sum(adjoint * (emission - incoming), axis=0, keepdims=True)
    stores[2].start()

    for copy in row_geom_out + col_geom_out + val_out + wt_out + fwd_out + ret_out:
        copy.wait_send()
    for copy in stores:
        copy.wait()


def finish(rad_ref, adj_ref, grad_ref, rad_hbm, adj_hbm, grad_hbm, sem):
    stores = [
        pltpu.make_async_copy(rad_ref, rad_hbm, sem.at[0]),
        pltpu.make_async_copy(adj_ref, adj_hbm, sem.at[1]),
        pltpu.make_async_copy(grad_ref, grad_hbm, sem.at[2]),
    ]
    for copy in stores:
        copy.start()
    for copy in stores:
        copy.wait()


def local(
    positions,
    angles,
    areas,
    emissivity,
    emission,
    radiosity_in,
    adjoint_in,
    visibility,
    inlet_patches,
    inlet_weights,
):
    emit_count = lax.axis_size("emit")
    recv_count = lax.axis_size("recv")
    own = areas.shape[0]
    cases = emission.shape[0]
    blocks = own // BLK
    row_total = own * recv_count
    group = math.gcd(recv_count, 4)
    hbm = pl.BlockSpec(memory_space=pltpu.HBM)
    emit_sem = pltpu.SemaphoreType.DMA((emit_count,))
    recv_sem = pltpu.SemaphoreType.DMA((recv_count,))
    operands = (
        positions,
        angles,
        areas[None, :],
        emissivity[None, :],
        radiosity_in,
        adjoint_in,
        visibility,
        inlet_patches[None, :],
        inlet_weights,
        emission,
    )
    flat = jax.ShapeDtypeStruct((cases, own), F32)
    results = (flat, flat, jax.ShapeDtypeStruct((1, own), F32))
    swept = pl.pallas_call(
        functools.partial(sweep, emit_count, recv_count),
        out_shape=results,
        in_specs=[hbm] * len(operands),
        out_specs=(hbm,) * 3,
        scratch_shapes=[pltpu.VMEM(x.shape, x.dtype) for x in operands]
        + [pltpu.VMEM(x.shape, x.dtype) for x in results]
        + [
            pltpu.SemaphoreType.DMA((len(operands),)),
            pltpu.SemaphoreType.DMA((3,)),
            pltpu.VMEM((recv_count, 8, own), F32),
            pltpu.VMEM((emit_count, 8, own), F32),
            pltpu.VMEM((recv_count, cases, own), BF16),
            pltpu.VMEM((emit_count, cases, own), BF16),
            pltpu.VMEM((emit_count * blocks, row_total), F32),
            pltpu.VMEM((recv_count, 48, own), BF16),
            pltpu.VMEM((recv_count, 48, own), BF16),
            pltpu.VMEM((recv_count, 48, own), BF16),
            pltpu.VMEM((own, own * group), BF16),
            pltpu.VMEM((row_total, cases), BF16),
            pltpu.VMEM((emit_count, cases, own), F32),
            pltpu.VMEM((emit_count, cases, own), F32),
            pltpu.VMEM((recv_count, cases, own), F32),
            pltpu.VMEM((recv_count, cases, own), F32),
            recv_sem,
            recv_sem,
            emit_sem,
            emit_sem,
            recv_sem,
            recv_sem,
            emit_sem,
            emit_sem,
            emit_sem,
            emit_sem,
            recv_sem,
            recv_sem,
        ],
        compiler_params=pltpu.CompilerParams(
            collective_id=0, has_side_effects=True, vmem_limit_bytes=64 * 1024 * 1024
        ),
        name="sweep",
    )(*operands)
    radiosity_out, adjoint_out, grad = pl.pallas_call(
        finish,
        out_shape=results,
        in_specs=[hbm] * 3,
        out_specs=(hbm,) * 3,
        scratch_shapes=[pltpu.SemaphoreType.DMA((3,))],
        compiler_params=pltpu.CompilerParams(vmem_limit_bytes=64 * 1024 * 1024),
        name="finish",
    )(*swept)
    return (radiosity_out, adjoint_out, grad[0])


def solution(mesh):
    placed = (
        P(None, ("groups", "emit", "recv")),
        P(None, ("groups", "emit", "recv")),
        P(("groups", "emit", "recv")),
        P(("groups", "emit", "recv")),
        P(None, ("groups", "emit", "recv")),
        P(None, ("groups", "emit", "recv")),
        P(None, ("groups", "emit", "recv")),
        P(("groups", "emit"), None),
        P("groups"),
        P(None, "groups"),
    )
    return jax.shard_map(
        local,
        mesh=mesh,
        in_specs=placed,
        out_specs=(
            P(None, ("groups", "emit", "recv")),
            P(None, ("groups", "emit", "recv")),
            P(("groups", "emit", "recv")),
        ),
        check_vma=False,
    )
```

```python
import functools
import math

import jax
import jax.numpy as jnp
from jax import lax
from jax.experimental import pallas as pl
from jax.experimental.pallas import tpu as pltpu
from jax.sharding import PartitionSpec as P

BLK = 128
MESH = pl.DeviceIdType.MESH
F32 = jnp.float32
BF16 = jnp.bfloat16


def flip(index, number):
    bit = 1
    while bit <= number:
        if number & bit:
            index = index + bit * (1 - 2 * ((index // bit) % 2))
        bit *= 2
    return index


def partner(index, number, count):
    if count & (count - 1) == 0:
        return flip(index, number)
    return lax.rem(index + number, count)


def split3(x):
    one = x.astype(BF16).astype(F32)
    rest = x - one
    two = rest.astype(BF16).astype(F32)
    return one, two, rest - two


def dot(a, b, ca, cb):
    return lax.dot_general(a, b, (((ca,), (cb,)), ((), ())), preferred_element_type=F32)


def sine_cosine(angles):
    half = 0.5 * angles
    square = half * half
    sine = jnp.full_like(half, 1.0 / math.factorial(13))
    cosine = jnp.full_like(half, 1.0 / math.factorial(14))
    cosine = cosine * square - 1.0 / math.factorial(12)
    for order in (11, 9, 7, 5, 3, 1):
        sign = -1.0 if order % 4 == 3 else 1.0
        sine = sine * square + sign / math.factorial(order)
        cosine = cosine * square - sign / math.factorial(order - 1)
    sine = sine * half
    cosine = -cosine
    return 2.0 * sine * cosine, 1.0 - 2.0 * sine * sine


def own_blocks_of(q, angles, area):
    sines, cosines = sine_cosine(angles)
    normal = jnp.concatenate(
        [sines[0:1] * cosines[1:2], sines[0:1] * sines[1:2], cosines[0:1]], axis=0
    )
    offset = -jnp.sum(normal * q, axis=0, keepdims=True)
    square = jnp.sum(q * q, axis=0, keepdims=True)
    scale = area * (1.0 / math.pi)
    emitter = jnp.concatenate([normal * scale, offset * scale, q, square + area], axis=0)
    receiver = jnp.concatenate([normal, offset, q, square], axis=0)
    return emitter, receiver


def emitter_forms(block):
    parts = split3(block)
    row = lax.broadcasted_iota(jnp.int32, block.shape, 0)
    order = (0, 0, 1, 1, 0, 2)
    stacks = []
    for place in (None, 7, 3):
        form = parts
        if place is not None:
            form = [jnp.where(row == place, float(n == 0), part) for n, part in enumerate(parts)]
        stacks.append(jnp.concatenate([form[n] for n in order], axis=0))
    return stacks


def receiver_forms(block):
    row = lax.broadcasted_iota(jnp.int32, block.shape, 0)
    turned = jnp.concatenate([block[4:8], block[0:4]], axis=0)
    cos_emit, cos_recv, spread = [], [], []
    for n, (part, swapped) in enumerate(zip(split3(block), split3(turned))):
        one = float(n == 0)
        cos_emit.append(jnp.where(row < 3, swapped, jnp.where(row == 3, one, 0.0)))
        cos_recv.append(jnp.where(row >= 4, swapped, 0.0))
        inner = jnp.where(row == 7, one, -2.0 * part)
        spread.append(jnp.where(row == 3, swapped, jnp.where(row >= 4, inner, 0.0)))
    order = (0, 1, 0, 1, 2, 0)
    return [
        jnp.concatenate([form[n] for n in order], axis=0) for form in (cos_emit, cos_recv, spread)
    ]


def sweep(
    emit_count,
    recv_count,
    pos_hbm,
    ang_hbm,
    area_hbm,
    emis_hbm,
    rad_hbm,
    adj_hbm,
    vis_hbm,
    inlet_hbm,
    weight_hbm,
    emission_hbm,
    rad_out_hbm,
    adj_out_hbm,
    grad_out_hbm,
    pos_ref,
    ang_ref,
    area_ref,
    emis_ref,
    rad_ref,
    adj_ref,
    vis_ref,
    inlet_ref,
    weight_ref,
    emission_ref,
    out_rad,
    out_adj,
    out_grad,
    load_sem,
    store_sem,
    row_geom,
    col_geom,
    row_val,
    col_wt,
    mask,
    form_a,
    form_b,
    form_s,
    tile,
    value_t,
    fwd_part,
    fwd_got,
    adj_part,
    adj_got,
    geom_row_send,
    geom_row_recv,
    geom_col_send,
    geom_col_recv,
    val_send,
    val_recv,
    wt_send,
    wt_recv,
    fwd_send,
    fwd_recv,
    ret_send,
    ret_recv,
):
    e = lax.axis_index("emit")
    r = lax.axis_index("recv")
    own = pos_ref.shape[1]
    blocks = own // BLK
    row_total = own * recv_count

    barrier = pltpu.get_barrier_semaphore()
    for k in range(1, recv_count):
        pl.semaphore_signal(
            barrier, inc=1, device_id={"recv": partner(r, k, recv_count)}, device_id_type=MESH
        )
    for k in range(1, emit_count):
        pl.semaphore_signal(
            barrier, inc=1, device_id={"emit": partner(e, k, emit_count)}, device_id_type=MESH
        )

    loads = [
        pltpu.make_async_copy(src, dst, load_sem.at[number])
        for number, (src, dst) in enumerate(
            (
                (pos_hbm, pos_ref),
                (ang_hbm, ang_ref),
                (area_hbm, area_ref),
                (emis_hbm, emis_ref),
                (rad_hbm, rad_ref),
                (adj_hbm, adj_ref),
                (vis_hbm, vis_ref),
                (inlet_hbm, inlet_ref),
                (weight_hbm, weight_ref),
                (emission_hbm, emission_ref),
            )
        )
    ]
    stores = [
        pltpu.make_async_copy(src, dst, store_sem.at[number])
        for number, (src, dst) in enumerate(
            (
                (out_rad, rad_out_hbm),
                (out_adj, adj_out_hbm),
                (out_grad, grad_out_hbm),
            )
        )
    ]
    for load in loads:
        load.start()

    for load in loads[:3]:
        load.wait()
    emitter, receiver = own_blocks_of(pos_ref[...] - 0.5, ang_ref[...], area_ref[...])
    row_geom[r] = emitter
    col_geom[e] = receiver

    pl.semaphore_wait(barrier, recv_count + emit_count - 2)

    def copies(buf, dst, send, recv, axis, me, count, gather):
        out = []
        for k in range(1, count):
            peer = partner(me, k, count)
            out.append(
                pltpu.make_async_remote_copy(
                    src_ref=buf.at[me if gather else peer],
                    dst_ref=dst.at[me],
                    send_sem=send.at[peer],
                    recv_sem=recv.at[me],
                    device_id={axis: peer},
                    device_id_type=MESH,
                )
            )
        return out

    def arrival(dst, send, recv, axis, peer):
        return pltpu.make_async_remote_copy(
            src_ref=dst.at[peer],
            dst_ref=dst.at[peer],
            send_sem=send.at[peer],
            recv_sem=recv.at[peer],
            device_id={axis: peer},
            device_id_type=MESH,
        )

    row_geom_out = copies(row_geom, row_geom, geom_row_send, geom_row_recv, "recv", r, recv_count, True)
    col_geom_out = copies(col_geom, col_geom, geom_col_send, geom_col_recv, "emit", e, emit_count, True)
    for copy in col_geom_out + row_geom_out:
        copy.start()
    for load in loads[3:6]:
        load.wait()
    row_val[r] = rad_ref[...].astype(BF16)
    col_wt[e] = ((1.0 - emis_ref[...]) * adj_ref[...]).astype(BF16)
    val_out = copies(row_val, row_val, val_send, val_recv, "recv", r, recv_count, True)
    wt_out = copies(col_wt, col_wt, wt_send, wt_recv, "emit", e, emit_count, True)
    for copy in wt_out + val_out:
        copy.start()

    loads[6].wait()
    all_blocks = vis_ref.shape[1]
    col_blocks = emit_count * blocks
    number = lax.broadcasted_iota(jnp.int32, (col_blocks, all_blocks), 0)
    wanted = (lax.div(number, blocks) * recv_count + r) * blocks + lax.rem(number, blocks)
    chosen = (lax.broadcasted_iota(jnp.int32, (col_blocks, all_blocks), 1) == wanted).astype(F32)
    tile_mask = dot(chosen.astype(BF16), vis_ref[...].astype(F32).astype(BF16), 1, 1)
    row_blocks = recv_count * blocks
    spot = lax.broadcasted_iota(jnp.int32, (row_blocks, row_total), 1) // BLK
    expand = (lax.broadcasted_iota(jnp.int32, (row_blocks, row_total), 0) == spot).astype(F32)
    mask[...] = dot(tile_mask.astype(BF16), expand.astype(BF16), 1, 0)

    for k in range(recv_count):
        peer = partner(r, k, recv_count)
        if k:
            arrival(row_geom, geom_row_send, geom_row_recv, "recv", peer).wait_recv()
        for form, buf in zip(emitter_forms(row_geom[peer]), (form_a, form_b, form_s)):
            buf[peer] = form.astype(BF16)

    lane = lax.broadcasted_iota(jnp.int32, (1, own), 1) // BLK
    group = tile.shape[1] // own

    def columns(peers, first):
        side_a, side_b, side_s = [], [], []
        for peer in peers:
            forms = receiver_forms(col_geom[peer])
            spaced = jnp.concatenate(
                [jnp.where(lane == b, forms[0], 0.0) for b in range(blocks)], axis=0
            )
            side_a.append(spaced.astype(BF16).T)
            side_b.append(forms[1].astype(BF16).T)
            side_s.append(forms[2].astype(BF16).T)
        side_b = jnp.concatenate(side_b, axis=0)
        side_s = jnp.concatenate(side_s, axis=0)
        weight = jnp.concatenate([col_wt[peer] for peer in peers], axis=1)
        height = own * len(peers)

        def rows(chunk, total):
            for inner in range(group):
                number = chunk * group + inner
                start = pl.multiple_of(number * own, own)
                base = form_a[number]
                across = slice(inner * own, (inner + 1) * own)
                cos_recv = jnp.maximum(dot(side_b, form_b[number], 1, 0), 0.0)
                spread = dot(side_s, form_s[number], 1, 0)
                ratio = cos_recv * pl.reciprocal(spread * spread, approx=True)
                for n, peer in enumerate(peers):
                    masked = jnp.concatenate(
                        [
                            base * mask[pl.ds(peer * blocks + b, 1), pl.ds(start, own)].astype(BF16)
                            for b in range(blocks)
                        ],
                        axis=0,
                    )
                    cos_emit = jnp.maximum(dot(side_a[n], masked, 1, 0), 0.0)
                    down = slice(n * own, (n + 1) * own)
                    tile[down, across] = (cos_emit * ratio[down]).astype(BF16)
            whole = tile[:height, :]
            back = dot(weight, whole, 1, 0)
            for inner in range(group):
                number = chunk * group + inner
                piece = back[:, inner * own : (inner + 1) * own]
                adj_part[number] = piece if first else adj_part[number] + piece
            width = group * own
            value = value_t[pl.ds(pl.multiple_of(chunk * width, width), width), :]
            return total + dot(whole, value, 1, 0)

        total = jnp.zeros((height, value_t.shape[1]), F32)
        if recv_count == group:
            total = rows(0, total)
        else:
            total = lax.fori_loop(0, recv_count // group, rows, total)
        for n, peer in enumerate(peers):
            fwd_part[peer] = total[n * own : (n + 1) * own].T

    for k in range(1, recv_count):
        arrival(row_val, val_send, val_recv, "recv", partner(r, k, recv_count)).wait_recv()
    for k in range(recv_count):
        value_t[k * own : (k + 1) * own, :] = row_val[k].T

    fwd_out = copies(fwd_part, fwd_got, fwd_send, fwd_recv, "emit", e, emit_count, False)
    together = tile.shape[0] // own
    for low in range(1, emit_count, together):
        numbers = range(low, min(low + together, emit_count))
        peers = [partner(e, k, emit_count) for k in numbers]
        for peer in peers:
            arrival(col_geom, geom_col_send, geom_col_recv, "emit", peer).wait_recv()
            arrival(col_wt, wt_send, wt_recv, "emit", peer).wait_recv()
        columns(peers, low == 1)
        for k in numbers:
            fwd_out[k - 1].start()
    columns([e], emit_count == 1)

    ret_out = copies(adj_part, adj_got, ret_send, ret_recv, "recv", r, recv_count, False)
    for copy in ret_out:
        copy.start()

    for load in loads[7:]:
        load.wait()
    patch = (e * recv_count + r) * own + lax.broadcasted_iota(jnp.int32, (own, 1), 0)
    selector = jnp.where(inlet_ref[...] == patch, 1.0, 0.0).astype(BF16)
    weights = weight_ref[...]
    high = weights.astype(BF16)
    low = (weights - high.astype(F32)).astype(BF16)
    source = dot(high, selector, 1, 1) + dot(low, selector, 1, 1)

    share = emis_ref[...]
    emission = emission_ref[...]

    incoming = fwd_part[e]
    for k in range(1, emit_count):
        peer = partner(e, k, emit_count)
        arrival(fwd_got, fwd_send, fwd_recv, "emit", peer).wait_recv()
        incoming = incoming + fwd_got[peer]
    out_rad[...] = share * emission + (1.0 - share) * incoming
    stores[0].start()
    returned = adj_part[r]
    for k in range(1, recv_count):
        peer = partner(r, k, recv_count)
        arrival(adj_got, ret_send, ret_recv, "recv", peer).wait_recv()
        returned = returned + adj_got[peer]
    adjoint = source + returned
    out_adj[...] = adjoint
    stores[1].start()
    out_grad[...] = jnp.sum(adjoint * (emission - incoming), axis=0, keepdims=True)
    stores[2].start()

    for copy in row_geom_out + col_geom_out + val_out + wt_out + fwd_out + ret_out:
        copy.wait_send()
    for copy in stores:
        copy.wait()


def finish(rad_in, adj_in, grad_in, rad_out, adj_out, grad_out, rad, adj, grad, load_sem, store_sem):
    loads, stores = [], []
    for n, (src, held, dst) in enumerate(
        ((rad_in, rad, rad_out), (adj_in, adj, adj_out), (grad_in, grad, grad_out))
    ):
        loads.append(pltpu.make_async_copy(src, held, load_sem.at[n]))
        stores.append(pltpu.make_async_copy(held, dst, store_sem.at[n]))
    for load in loads:
        load.start()
    for load, store in zip(loads, stores):
        load.wait()
        store.start()
    for store in stores:
        store.wait()


def local(
    positions,
    angles,
    areas,
    emissivity,
    emission,
    radiosity_in,
    adjoint_in,
    visibility,
    inlet_patches,
    inlet_weights,
):
    emit_count = lax.axis_size("emit")
    recv_count = lax.axis_size("recv")
    own = areas.shape[0]
    cases = emission.shape[0]
    blocks = own // BLK
    row_total = own * recv_count
    group = math.gcd(recv_count, 4)
    hbm = pl.BlockSpec(memory_space=pltpu.HBM)
    emit_sem = pltpu.SemaphoreType.DMA((emit_count,))
    recv_sem = pltpu.SemaphoreType.DMA((recv_count,))
    operands = (
        positions,
        angles,
        areas[None, :],
        emissivity[None, :],
        radiosity_in,
        adjoint_in,
        visibility,
        inlet_patches[None, :],
        inlet_weights,
        emission,
    )
    flat = jax.ShapeDtypeStruct((cases, own), F32)
    results = (flat, flat, jax.ShapeDtypeStruct((1, own), F32))
    swept = pl.pallas_call(
        functools.partial(sweep, emit_count, recv_count),
        out_shape=results,
        in_specs=[hbm] * len(operands),
        out_specs=(hbm,) * 3,
        scratch_shapes=[pltpu.VMEM(x.shape, x.dtype) for x in operands]
        + [pltpu.VMEM(x.shape, x.dtype) for x in results]
        + [
            pltpu.SemaphoreType.DMA((len(operands),)),
            pltpu.SemaphoreType.DMA((3,)),
            pltpu.VMEM((recv_count, 8, own), F32),
            pltpu.VMEM((emit_count, 8, own), F32),
            pltpu.VMEM((recv_count, cases, own), BF16),
            pltpu.VMEM((emit_count, cases, own), BF16),
            pltpu.VMEM((emit_count * blocks, row_total), F32),
            pltpu.VMEM((recv_count, 48, own), BF16),
            pltpu.VMEM((recv_count, 48, own), BF16),
            pltpu.VMEM((recv_count, 48, own), BF16),
            pltpu.VMEM((own * max(1, min(3, emit_count - 1)), own * group), BF16),
            pltpu.VMEM((row_total, cases), BF16),
            pltpu.VMEM((emit_count, cases, own), F32),
            pltpu.VMEM((emit_count, cases, own), F32),
            pltpu.VMEM((recv_count, cases, own), F32),
            pltpu.VMEM((recv_count, cases, own), F32),
            recv_sem,
            recv_sem,
            emit_sem,
            emit_sem,
            recv_sem,
            recv_sem,
            emit_sem,
            emit_sem,
            emit_sem,
            emit_sem,
            recv_sem,
            recv_sem,
        ],
        compiler_params=pltpu.CompilerParams(
            collective_id=0, has_side_effects=True, vmem_limit_bytes=64 * 1024 * 1024
        ),
        name="sweep",
    )(*operands)
    radiosity_out, adjoint_out, grad = pl.pallas_call(
        finish,
        out_shape=results,
        in_specs=[hbm] * 3,
        out_specs=(hbm,) * 3,
        scratch_shapes=[pltpu.VMEM(x.shape, x.dtype) for x in results]
        + [pltpu.SemaphoreType.DMA((3,)), pltpu.SemaphoreType.DMA((3,))],
        compiler_params=pltpu.CompilerParams(vmem_limit_bytes=64 * 1024 * 1024),
        name="finish",
    )(*swept)
    return (radiosity_out, adjoint_out, grad[0])


def solution(mesh):
    placed = (
        P(None, ("groups", "emit", "recv")),
        P(None, ("groups", "emit", "recv")),
        P(("groups", "emit", "recv")),
        P(("groups", "emit", "recv")),
        P(None, ("groups", "emit", "recv")),
        P(None, ("groups", "emit", "recv")),
        P(None, ("groups", "emit", "recv")),
        P(("groups", "emit"), None),
        P("groups"),
        P(None, "groups"),
    )
    return jax.shard_map(
        local,
        mesh=mesh,
        in_specs=placed,
        out_specs=(
            P(None, ("groups", "emit", "recv")),
            P(None, ("groups", "emit", "recv")),
            P(("groups", "emit", "recv")),
        ),
        check_vma=False,
    )
```

```python
import functools
import math

import jax
import jax.numpy as jnp
from jax import lax
from jax.experimental import pallas as pl
from jax.experimental.pallas import tpu as pltpu
from jax.sharding import PartitionSpec as P

BLK = 128
MESH = pl.DeviceIdType.MESH
F32 = jnp.float32
BF16 = jnp.bfloat16


def flip(index, number):
    bit = 1
    while bit <= number:
        if number & bit:
            index = index + bit * (1 - 2 * ((index // bit) % 2))
        bit *= 2
    return index


def partner(index, number, count):
    if count & (count - 1) == 0:
        return flip(index, number)
    return lax.rem(index + number, count)


def split3(x):
    one = x.astype(BF16).astype(F32)
    rest = x - one
    two = rest.astype(BF16).astype(F32)
    return one, two, rest - two


def dot(a, b, ca, cb):
    return lax.dot_general(a, b, (((ca,), (cb,)), ((), ())), preferred_element_type=F32)


def sine_cosine(angles):
    half = 0.5 * angles
    square = half * half
    sine = jnp.full_like(half, 1.0 / math.factorial(13))
    cosine = jnp.full_like(half, 1.0 / math.factorial(14))
    cosine = cosine * square - 1.0 / math.factorial(12)
    for order in (11, 9, 7, 5, 3, 1):
        sign = -1.0 if order % 4 == 3 else 1.0
        sine = sine * square + sign / math.factorial(order)
        cosine = cosine * square - sign / math.factorial(order - 1)
    sine = sine * half
    cosine = -cosine
    return 2.0 * sine * cosine, 1.0 - 2.0 * sine * sine


def own_blocks_of(q, angles, area):
    sines, cosines = sine_cosine(angles)
    normal = jnp.concatenate(
        [sines[0:1] * cosines[1:2], sines[0:1] * sines[1:2], cosines[0:1]], axis=0
    )
    offset = -jnp.sum(normal * q, axis=0, keepdims=True)
    square = jnp.sum(q * q, axis=0, keepdims=True)
    scale = area * (1.0 / math.pi)
    emitter = jnp.concatenate([normal * scale, offset * scale, q, square + area], axis=0)
    receiver = jnp.concatenate([normal, offset, q, square], axis=0)
    return emitter, receiver


def emitter_forms(block):
    parts = split3(block)
    row = lax.broadcasted_iota(jnp.int32, block.shape, 0)
    order = (0, 0, 1, 1, 0, 2)
    stacks = []
    for place in (None, 7, 3):
        form = parts
        if place is not None:
            form = [jnp.where(row == place, float(n == 0), part) for n, part in enumerate(parts)]
        stacks.append(jnp.concatenate([form[n] for n in order], axis=0))
    return stacks


def receiver_forms(block):
    row = lax.broadcasted_iota(jnp.int32, block.shape, 0)
    turned = jnp.concatenate([block[4:8], block[0:4]], axis=0)
    cos_emit, cos_recv, spread = [], [], []
    for n, (part, swapped) in enumerate(zip(split3(block), split3(turned))):
        one = float(n == 0)
        cos_emit.append(jnp.where(row < 3, swapped, jnp.where(row == 3, one, 0.0)))
        cos_recv.append(jnp.where(row >= 4, swapped, 0.0))
        inner = jnp.where(row == 7, one, -2.0 * part)
        spread.append(jnp.where(row == 3, swapped, jnp.where(row >= 4, inner, 0.0)))
    order = (0, 1, 0, 1, 2, 0)
    return [
        jnp.concatenate([form[n] for n in order], axis=0) for form in (cos_emit, cos_recv, spread)
    ]


def sweep(
    emit_count,
    recv_count,
    pos_hbm,
    ang_hbm,
    area_hbm,
    emis_hbm,
    rad_hbm,
    adj_hbm,
    vis_hbm,
    inlet_hbm,
    weight_hbm,
    emission_hbm,
    rad_out_hbm,
    adj_out_hbm,
    grad_out_hbm,
    pos_ref,
    ang_ref,
    area_ref,
    emis_ref,
    rad_ref,
    adj_ref,
    vis_ref,
    inlet_ref,
    weight_ref,
    emission_ref,
    out_rad,
    out_adj,
    out_grad,
    load_sem,
    store_sem,
    row_geom,
    col_geom,
    row_val,
    col_wt,
    mask,
    form_a,
    form_b,
    form_s,
    tile,
    value_t,
    fwd_part,
    fwd_got,
    adj_part,
    adj_got,
    geom_row_send,
    geom_row_recv,
    geom_col_send,
    geom_col_recv,
    val_send,
    val_recv,
    wt_send,
    wt_recv,
    fwd_send,
    fwd_recv,
    ret_send,
    ret_recv,
):
    e = lax.axis_index("emit")
    r = lax.axis_index("recv")
    own = pos_ref.shape[1]
    blocks = own // BLK
    row_total = own * recv_count

    barrier = pltpu.get_barrier_semaphore()
    for k in range(1, recv_count):
        pl.semaphore_signal(
            barrier, inc=1, device_id={"recv": partner(r, k, recv_count)}, device_id_type=MESH
        )
    for k in range(1, emit_count):
        pl.semaphore_signal(
            barrier, inc=1, device_id={"emit": partner(e, k, emit_count)}, device_id_type=MESH
        )

    loads = [
        pltpu.make_async_copy(src, dst, load_sem.at[number])
        for number, (src, dst) in enumerate(
            (
                (pos_hbm, pos_ref),
                (ang_hbm, ang_ref),
                (area_hbm, area_ref),
                (emis_hbm, emis_ref),
                (rad_hbm, rad_ref),
                (adj_hbm, adj_ref),
                (vis_hbm, vis_ref),
                (inlet_hbm, inlet_ref),
                (weight_hbm, weight_ref),
                (emission_hbm, emission_ref),
            )
        )
    ]
    stores = [
        pltpu.make_async_copy(src, dst, store_sem.at[number])
        for number, (src, dst) in enumerate(
            (
                (out_rad, rad_out_hbm),
                (out_adj, adj_out_hbm),
                (out_grad, grad_out_hbm),
            )
        )
    ]
    for load in loads:
        load.start()

    for load in loads[:3]:
        load.wait()
    emitter, receiver = own_blocks_of(pos_ref[...] - 0.5, ang_ref[...], area_ref[...])
    row_geom[r] = emitter
    col_geom[e] = receiver

    pl.semaphore_wait(barrier, recv_count + emit_count - 2)

    def copies(buf, dst, send, recv, axis, me, count, gather):
        out = []
        for k in range(1, count):
            peer = partner(me, k, count)
            out.append(
                pltpu.make_async_remote_copy(
                    src_ref=buf.at[me if gather else peer],
                    dst_ref=dst.at[me],
                    send_sem=send.at[peer],
                    recv_sem=recv.at[me],
                    device_id={axis: peer},
                    device_id_type=MESH,
                )
            )
        return out

    def arrival(dst, send, recv, axis, peer):
        return pltpu.make_async_remote_copy(
            src_ref=dst.at[peer],
            dst_ref=dst.at[peer],
            send_sem=send.at[peer],
            recv_sem=recv.at[peer],
            device_id={axis: peer},
            device_id_type=MESH,
        )

    row_geom_out = copies(row_geom, row_geom, geom_row_send, geom_row_recv, "recv", r, recv_count, True)
    col_geom_out = copies(col_geom, col_geom, geom_col_send, geom_col_recv, "emit", e, emit_count, True)
    for copy in col_geom_out + row_geom_out:
        copy.start()
    for load in loads[3:6]:
        load.wait()
    row_val[r] = rad_ref[...].astype(BF16)
    col_wt[e] = ((1.0 - emis_ref[...]) * adj_ref[...]).astype(BF16)
    val_out = copies(row_val, row_val, val_send, val_recv, "recv", r, recv_count, True)
    wt_out = copies(col_wt, col_wt, wt_send, wt_recv, "emit", e, emit_count, True)
    for copy in wt_out + val_out:
        copy.start()

    loads[6].wait()
    all_blocks = vis_ref.shape[1]
    col_blocks = emit_count * blocks
    number = lax.broadcasted_iota(jnp.int32, (col_blocks, all_blocks), 0)
    wanted = (lax.div(number, blocks) * recv_count + r) * blocks + lax.rem(number, blocks)
    chosen = (lax.broadcasted_iota(jnp.int32, (col_blocks, all_blocks), 1) == wanted).astype(F32)
    tile_mask = dot(chosen.astype(BF16), vis_ref[...].astype(F32).astype(BF16), 1, 1)
    row_blocks = recv_count * blocks
    spot = lax.broadcasted_iota(jnp.int32, (row_blocks, row_total), 1) // BLK
    expand = (lax.broadcasted_iota(jnp.int32, (row_blocks, row_total), 0) == spot).astype(F32)
    mask[...] = dot(tile_mask.astype(BF16), expand.astype(BF16), 1, 0)

    for k in range(recv_count):
        peer = partner(r, k, recv_count)
        if k:
            arrival(row_geom, geom_row_send, geom_row_recv, "recv", peer).wait_recv()
        for form, buf in zip(emitter_forms(row_geom[peer]), (form_a, form_b, form_s)):
            buf[peer] = form.astype(BF16)

    lane = lax.broadcasted_iota(jnp.int32, (1, own), 1) // BLK
    group = tile.shape[1] // own

    def columns(peer, first, last):
        forms = receiver_forms(col_geom[peer])
        spaced = jnp.concatenate([jnp.where(lane == b, forms[0], 0.0) for b in range(blocks)], axis=0)
        side_a = spaced.astype(BF16).T
        side_b = forms[1].astype(BF16).T
        side_s = forms[2].astype(BF16).T
        weight = col_wt[peer]

        def rows(chunk, total):
            for inner in range(group):
                number = chunk * group + inner
                start = pl.multiple_of(number * own, own)
                base = form_a[number]
                masked = jnp.concatenate(
                    [
                        base * mask[pl.ds(peer * blocks + b, 1), pl.ds(start, own)].astype(BF16)
                        for b in range(blocks)
                    ],
                    axis=0,
                )
                cos_emit = jnp.maximum(dot(side_a, masked, 1, 0), 0.0)
                cos_recv = jnp.maximum(dot(side_b, form_b[number], 1, 0), 0.0)
                spread = dot(side_s, form_s[number], 1, 0)
                tile[:, inner * own : (inner + 1) * own] = (
                    cos_emit * cos_recv * pl.reciprocal(spread * spread, approx=True)
                ).astype(BF16)
            whole = tile[...]
            back = dot(weight, whole, 1, 0)
            for inner in range(group):
                number = chunk * group + inner
                piece = back[:, inner * own : (inner + 1) * own]
                adj_part[number] = piece if first else adj_part[number] + piece
            if last and recv_count == group:
                for copy in ret_out:
                    copy.start()
            width = group * own
            value = value_t[pl.ds(pl.multiple_of(chunk * width, width), width), :]
            return total + dot(whole, value, 1, 0)

        total = jnp.zeros((own, value_t.shape[1]), F32)
        if recv_count == group:
            total = rows(0, total)
        else:
            total = lax.fori_loop(0, recv_count // group, rows, total)
        fwd_part[peer] = total.T
        if last and recv_count != group:
            for copy in ret_out:
                copy.start()

    for k in range(1, recv_count):
        arrival(row_val, val_send, val_recv, "recv", partner(r, k, recv_count)).wait_recv()
    for k in range(recv_count):
        value_t[k * own : (k + 1) * own, :] = row_val[k].T

    ret_out = copies(adj_part, adj_got, ret_send, ret_recv, "recv", r, recv_count, False)
    fwd_out = copies(fwd_part, fwd_got, fwd_send, fwd_recv, "emit", e, emit_count, False)
    columns(e, True, emit_count == 1)
    for k in reversed(range(1, emit_count)):
        peer = partner(e, k, emit_count)
        arrival(col_geom, geom_col_send, geom_col_recv, "emit", peer).wait_recv()
        arrival(col_wt, wt_send, wt_recv, "emit", peer).wait_recv()
        columns(peer, False, k == 1)
        fwd_out[k - 1].start()


    for load in loads[7:]:
        load.wait()
    patch = (e * recv_count + r) * own + lax.broadcasted_iota(jnp.int32, (own, 1), 0)
    selector = jnp.where(inlet_ref[...] == patch, 1.0, 0.0).astype(BF16)
    weights = weight_ref[...]
    high = weights.astype(BF16)
    low = (weights - high.astype(F32)).astype(BF16)
    source = dot(high, selector, 1, 1) + dot(low, selector, 1, 1)

    share = emis_ref[...]
    emission = emission_ref[...]

    incoming = fwd_part[e]
    for k in range(1, emit_count):
        peer = partner(e, k, emit_count)
        arrival(fwd_got, fwd_send, fwd_recv, "emit", peer).wait_recv()
        incoming = incoming + fwd_got[peer]
    out_rad[...] = share * emission + (1.0 - share) * incoming
    stores[0].start()
    returned = adj_part[r]
    for k in range(1, recv_count):
        peer = partner(r, k, recv_count)
        arrival(adj_got, ret_send, ret_recv, "recv", peer).wait_recv()
        returned = returned + adj_got[peer]
    adjoint = source + returned
    out_adj[...] = adjoint
    stores[1].start()
    out_grad[...] = jnp.sum(adjoint * (emission - incoming), axis=0, keepdims=True)
    stores[2].start()

    for copy in row_geom_out + col_geom_out + val_out + wt_out + fwd_out + ret_out:
        copy.wait_send()
    for copy in stores:
        copy.wait()


def finish(rad_in, adj_in, grad_in, rad_out, adj_out, grad_out, rad, adj, grad, load_sem, store_sem):
    loads, stores = [], []
    for n, (src, held, dst) in enumerate(
        ((rad_in, rad, rad_out), (adj_in, adj, adj_out), (grad_in, grad, grad_out))
    ):
        loads.append(pltpu.make_async_copy(src, held, load_sem.at[n]))
        stores.append(pltpu.make_async_copy(held, dst, store_sem.at[n]))
    for load in loads:
        load.start()
    for load, store in zip(loads, stores):
        load.wait()
        store.start()
    for store in stores:
        store.wait()


def local(
    positions,
    angles,
    areas,
    emissivity,
    emission,
    radiosity_in,
    adjoint_in,
    visibility,
    inlet_patches,
    inlet_weights,
):
    emit_count = lax.axis_size("emit")
    recv_count = lax.axis_size("recv")
    own = areas.shape[0]
    cases = emission.shape[0]
    blocks = own // BLK
    row_total = own * recv_count
    group = math.gcd(recv_count, 4)
    hbm = pl.BlockSpec(memory_space=pltpu.HBM)
    emit_sem = pltpu.SemaphoreType.DMA((emit_count,))
    recv_sem = pltpu.SemaphoreType.DMA((recv_count,))
    operands = (
        positions,
        angles,
        areas[None, :],
        emissivity[None, :],
        radiosity_in,
        adjoint_in,
        visibility,
        inlet_patches[None, :],
        inlet_weights,
        emission,
    )
    flat = jax.ShapeDtypeStruct((cases, own), F32)
    results = (flat, flat, jax.ShapeDtypeStruct((1, own), F32))
    swept = pl.pallas_call(
        functools.partial(sweep, emit_count, recv_count),
        out_shape=results,
        in_specs=[hbm] * len(operands),
        out_specs=(hbm,) * 3,
        scratch_shapes=[pltpu.VMEM(x.shape, x.dtype) for x in operands]
        + [pltpu.VMEM(x.shape, x.dtype) for x in results]
        + [
            pltpu.SemaphoreType.DMA((len(operands),)),
            pltpu.SemaphoreType.DMA((3,)),
            pltpu.VMEM((recv_count, 8, own), F32),
            pltpu.VMEM((emit_count, 8, own), F32),
            pltpu.VMEM((recv_count, cases, own), BF16),
            pltpu.VMEM((emit_count, cases, own), BF16),
            pltpu.VMEM((emit_count * blocks, row_total), F32),
            pltpu.VMEM((recv_count, 48, own), BF16),
            pltpu.VMEM((recv_count, 48, own), BF16),
            pltpu.VMEM((recv_count, 48, own), BF16),
            pltpu.VMEM((own, own * group), BF16),
            pltpu.VMEM((row_total, cases), BF16),
            pltpu.VMEM((emit_count, cases, own), F32),
            pltpu.VMEM((emit_count, cases, own), F32),
            pltpu.VMEM((recv_count, cases, own), F32),
            pltpu.VMEM((recv_count, cases, own), F32),
            recv_sem,
            recv_sem,
            emit_sem,
            emit_sem,
            recv_sem,
            recv_sem,
            emit_sem,
            emit_sem,
            emit_sem,
            emit_sem,
            recv_sem,
            recv_sem,
        ],
        compiler_params=pltpu.CompilerParams(
            collective_id=0, has_side_effects=True, vmem_limit_bytes=64 * 1024 * 1024
        ),
        name="sweep",
    )(*operands)
    radiosity_out, adjoint_out, grad = pl.pallas_call(
        finish,
        out_shape=results,
        in_specs=[hbm] * 3,
        out_specs=(hbm,) * 3,
        scratch_shapes=[pltpu.VMEM(x.shape, x.dtype) for x in results]
        + [pltpu.SemaphoreType.DMA((3,)), pltpu.SemaphoreType.DMA((3,))],
        compiler_params=pltpu.CompilerParams(vmem_limit_bytes=64 * 1024 * 1024),
        name="finish",
    )(*swept)
    return (radiosity_out, adjoint_out, grad[0])


def solution(mesh):
    placed = (
        P(None, ("groups", "emit", "recv")),
        P(None, ("groups", "emit", "recv")),
        P(("groups", "emit", "recv")),
        P(("groups", "emit", "recv")),
        P(None, ("groups", "emit", "recv")),
        P(None, ("groups", "emit", "recv")),
        P(None, ("groups", "emit", "recv")),
        P(("groups", "emit"), None),
        P("groups"),
        P(None, "groups"),
    )
    return jax.shard_map(
        local,
        mesh=mesh,
        in_specs=placed,
        out_specs=(
            P(None, ("groups", "emit", "recv")),
            P(None, ("groups", "emit", "recv")),
            P(("groups", "emit", "recv")),
        ),
        check_vma=False,
    )
```

```python
import functools
import math

import jax
import jax.numpy as jnp
from jax import lax
from jax.experimental import pallas as pl
from jax.experimental.pallas import tpu as pltpu
from jax.sharding import PartitionSpec as P

BLK = 128
MESH = pl.DeviceIdType.MESH
F32 = jnp.float32
BF16 = jnp.bfloat16


def flip(index, number):
    bit = 1
    while bit <= number:
        if number & bit:
            index = index + bit * (1 - 2 * ((index // bit) % 2))
        bit *= 2
    return index


def partner(index, number, count):
    if count & (count - 1) == 0:
        return flip(index, number)
    return lax.rem(index + number, count)


def split3(x):
    one = x.astype(BF16).astype(F32)
    rest = x - one
    two = rest.astype(BF16).astype(F32)
    return one, two, rest - two


def dot(a, b, ca, cb):
    return lax.dot_general(a, b, (((ca,), (cb,)), ((), ())), preferred_element_type=F32)


def sine_cosine(angles):
    half = 0.5 * angles
    square = half * half
    sine = jnp.full_like(half, 1.0 / math.factorial(13))
    cosine = jnp.full_like(half, 1.0 / math.factorial(14))
    cosine = cosine * square - 1.0 / math.factorial(12)
    for order in (11, 9, 7, 5, 3, 1):
        sign = -1.0 if order % 4 == 3 else 1.0
        sine = sine * square + sign / math.factorial(order)
        cosine = cosine * square - sign / math.factorial(order - 1)
    sine = sine * half
    cosine = -cosine
    return 2.0 * sine * cosine, 1.0 - 2.0 * sine * sine


def own_blocks_of(q, angles, area):
    sines, cosines = sine_cosine(angles)
    normal = jnp.concatenate(
        [sines[0:1] * cosines[1:2], sines[0:1] * sines[1:2], cosines[0:1]], axis=0
    )
    offset = -jnp.sum(normal * q, axis=0, keepdims=True)
    square = jnp.sum(q * q, axis=0, keepdims=True)
    scale = area * (1.0 / math.pi)
    emitter = jnp.concatenate([normal * scale, offset * scale, q, square + area], axis=0)
    receiver = jnp.concatenate([normal, offset, q, square], axis=0)
    return emitter, receiver


def emitter_forms(block):
    parts = split3(block)
    row = lax.broadcasted_iota(jnp.int32, block.shape, 0)
    order = (0, 0, 1, 1, 0, 2)
    stacks = []
    for place in (None, 7, 3):
        form = parts
        if place is not None:
            form = [jnp.where(row == place, float(n == 0), part) for n, part in enumerate(parts)]
        stacks.append(jnp.concatenate([form[n] for n in order], axis=0))
    return stacks


def receiver_forms(block):
    row = lax.broadcasted_iota(jnp.int32, block.shape, 0)
    turned = jnp.concatenate([block[4:8], block[0:4]], axis=0)
    cos_emit, cos_recv, spread = [], [], []
    for n, (part, swapped) in enumerate(zip(split3(block), split3(turned))):
        one = float(n == 0)
        cos_emit.append(jnp.where(row < 3, swapped, jnp.where(row == 3, one, 0.0)))
        cos_recv.append(jnp.where(row >= 4, swapped, 0.0))
        inner = jnp.where(row == 7, one, -2.0 * part)
        spread.append(jnp.where(row == 3, swapped, jnp.where(row >= 4, inner, 0.0)))
    order = (0, 1, 0, 1, 2, 0)
    return [
        jnp.concatenate([form[n] for n in order], axis=0) for form in (cos_emit, cos_recv, spread)
    ]


def sweep(
    emit_count,
    recv_count,
    pos_hbm,
    ang_hbm,
    area_hbm,
    emis_hbm,
    rad_hbm,
    adj_hbm,
    vis_hbm,
    inlet_hbm,
    weight_hbm,
    emission_hbm,
    rad_out_hbm,
    adj_out_hbm,
    grad_out_hbm,
    pos_ref,
    ang_ref,
    area_ref,
    emis_ref,
    rad_ref,
    adj_ref,
    vis_ref,
    inlet_ref,
    weight_ref,
    emission_ref,
    out_rad,
    out_adj,
    out_grad,
    load_sem,
    store_sem,
    row_geom,
    col_geom,
    row_val,
    col_wt,
    mask,
    form_a,
    form_b,
    form_s,
    tile,
    value_t,
    fwd_part,
    fwd_got,
    adj_part,
    adj_got,
    geom_row_send,
    geom_row_recv,
    geom_col_send,
    geom_col_recv,
    val_send,
    val_recv,
    wt_send,
    wt_recv,
    fwd_send,
    fwd_recv,
    ret_send,
    ret_recv,
):
    e = lax.axis_index("emit")
    r = lax.axis_index("recv")
    own = pos_ref.shape[1]
    blocks = own // BLK
    row_total = own * recv_count

    barrier = pltpu.get_barrier_semaphore()
    for k in range(1, recv_count):
        pl.semaphore_signal(
            barrier, inc=1, device_id={"recv": partner(r, k, recv_count)}, device_id_type=MESH
        )
    for k in range(1, emit_count):
        pl.semaphore_signal(
            barrier, inc=1, device_id={"emit": partner(e, k, emit_count)}, device_id_type=MESH
        )

    loads = [
        pltpu.make_async_copy(src, dst, load_sem.at[number])
        for number, (src, dst) in enumerate(
            (
                (pos_hbm, pos_ref),
                (ang_hbm, ang_ref),
                (area_hbm, area_ref),
                (emis_hbm, emis_ref),
                (rad_hbm, rad_ref),
                (adj_hbm, adj_ref),
                (vis_hbm, vis_ref),
                (inlet_hbm, inlet_ref),
                (weight_hbm, weight_ref),
                (emission_hbm, emission_ref),
            )
        )
    ]
    stores = [
        pltpu.make_async_copy(src, dst, store_sem.at[number])
        for number, (src, dst) in enumerate(
            (
                (out_rad, rad_out_hbm),
                (out_adj, adj_out_hbm),
                (out_grad, grad_out_hbm),
            )
        )
    ]
    for load in loads:
        load.start()

    for load in loads[:3]:
        load.wait()
    emitter, receiver = own_blocks_of(pos_ref[...] - 0.5, ang_ref[...], area_ref[...])
    row_geom[r] = emitter
    col_geom[e] = receiver

    pl.semaphore_wait(barrier, recv_count + emit_count - 2)

    def copies(buf, dst, send, recv, axis, me, count, gather):
        out = []
        for k in range(1, count):
            peer = partner(me, k, count)
            out.append(
                pltpu.make_async_remote_copy(
                    src_ref=buf.at[me if gather else peer],
                    dst_ref=dst.at[me],
                    send_sem=send.at[peer],
                    recv_sem=recv.at[me],
                    device_id={axis: peer},
                    device_id_type=MESH,
                )
            )
        return out

    def arrival(dst, send, recv, axis, peer):
        return pltpu.make_async_remote_copy(
            src_ref=dst.at[peer],
            dst_ref=dst.at[peer],
            send_sem=send.at[peer],
            recv_sem=recv.at[peer],
            device_id={axis: peer},
            device_id_type=MESH,
        )

    row_geom_out = copies(row_geom, row_geom, geom_row_send, geom_row_recv, "recv", r, recv_count, True)
    col_geom_out = copies(col_geom, col_geom, geom_col_send, geom_col_recv, "emit", e, emit_count, True)
    for copy in row_geom_out + col_geom_out[::-1]:
        copy.start()
    for load in loads[3:6]:
        load.wait()
    row_val[r] = rad_ref[...].astype(BF16)
    col_wt[e] = ((1.0 - emis_ref[...]) * adj_ref[...]).astype(BF16)
    val_out = copies(row_val, row_val, val_send, val_recv, "recv", r, recv_count, True)
    wt_out = copies(col_wt, col_wt, wt_send, wt_recv, "emit", e, emit_count, True)
    for copy in val_out + wt_out[::-1]:
        copy.start()

    loads[6].wait()
    all_blocks = vis_ref.shape[1]
    col_blocks = emit_count * blocks
    number = lax.broadcasted_iota(jnp.int32, (col_blocks, all_blocks), 0)
    wanted = (lax.div(number, blocks) * recv_count + r) * blocks + lax.rem(number, blocks)
    chosen = (lax.broadcasted_iota(jnp.int32, (col_blocks, all_blocks), 1) == wanted).astype(F32)
    tile_mask = dot(chosen.astype(BF16), vis_ref[...].astype(F32).astype(BF16), 1, 1)
    row_blocks = recv_count * blocks
    spot = lax.broadcasted_iota(jnp.int32, (row_blocks, row_total), 1) // BLK
    expand = (lax.broadcasted_iota(jnp.int32, (row_blocks, row_total), 0) == spot).astype(F32)
    mask[...] = dot(tile_mask.astype(BF16), expand.astype(BF16), 1, 0)

    for k in range(recv_count):
        peer = partner(r, k, recv_count)
        if k:
            arrival(row_geom, geom_row_send, geom_row_recv, "recv", peer).wait_recv()
        for form, buf in zip(emitter_forms(row_geom[peer]), (form_a, form_b, form_s)):
            buf[peer] = form.astype(BF16)

    lane = lax.broadcasted_iota(jnp.int32, (1, own), 1) // BLK
    group = tile.shape[1] // own

    def values_ready():
        for k in range(1, recv_count):
            arrival(row_val, val_send, val_recv, "recv", partner(r, k, recv_count)).wait_recv()
        for k in range(recv_count):
            value_t[k * own : (k + 1) * own, :] = row_val[k].T

    if recv_count != group:
        values_ready()

    def columns(peer, first, last):
        forms = receiver_forms(col_geom[peer])
        spaced = jnp.concatenate([jnp.where(lane == b, forms[0], 0.0) for b in range(blocks)], axis=0)
        side_a = spaced.astype(BF16).T
        side_b = forms[1].astype(BF16).T
        side_s = forms[2].astype(BF16).T
        weight = col_wt[peer]

        def rows(chunk, total):
            for inner in range(group):
                number = chunk * group + inner
                start = pl.multiple_of(number * own, own)
                base = form_a[number]
                masked = jnp.concatenate(
                    [
                        base * mask[pl.ds(peer * blocks + b, 1), pl.ds(start, own)].astype(BF16)
                        for b in range(blocks)
                    ],
                    axis=0,
                )
                cos_emit = jnp.maximum(dot(side_a, masked, 1, 0), 0.0)
                cos_recv = jnp.maximum(dot(side_b, form_b[number], 1, 0), 0.0)
                spread = dot(side_s, form_s[number], 1, 0)
                tile[:, inner * own : (inner + 1) * own] = (
                    cos_emit * cos_recv * pl.reciprocal(spread * spread, approx=True)
                ).astype(BF16)
            if first and recv_count == group:
                values_ready()
            whole = tile[...]
            back = dot(weight, whole, 1, 0)
            for inner in range(group):
                number = chunk * group + inner
                piece = back[:, inner * own : (inner + 1) * own]
                adj_part[number] = piece if first else adj_part[number] + piece
            if last and recv_count == group:
                for copy in ret_out:
                    copy.start()
            width = group * own
            value = value_t[pl.ds(pl.multiple_of(chunk * width, width), width), :]
            return total + dot(whole, value, 1, 0)

        total = jnp.zeros((own, value_t.shape[1]), F32)
        if recv_count == group:
            total = rows(0, total)
        else:
            total = lax.fori_loop(0, recv_count // group, rows, total)
        fwd_part[peer] = total.T
        if last and recv_count != group:
            for copy in ret_out:
                copy.start()


    ret_out = copies(adj_part, adj_got, ret_send, ret_recv, "recv", r, recv_count, False)
    fwd_out = copies(fwd_part, fwd_got, fwd_send, fwd_recv, "emit", e, emit_count, False)
    columns(e, True, emit_count == 1)
    for k in reversed(range(1, emit_count)):
        peer = partner(e, k, emit_count)
        arrival(col_geom, geom_col_send, geom_col_recv, "emit", peer).wait_recv()
        arrival(col_wt, wt_send, wt_recv, "emit", peer).wait_recv()
        columns(peer, False, k == 1)
        fwd_out[k - 1].start()


    for load in loads[7:]:
        load.wait()
    patch = (e * recv_count + r) * own + lax.broadcasted_iota(jnp.int32, (own, 1), 0)
    selector = jnp.where(inlet_ref[...] == patch, 1.0, 0.0).astype(BF16)
    weights = weight_ref[...]
    high = weights.astype(BF16)
    low = (weights - high.astype(F32)).astype(BF16)
    source = dot(high, selector, 1, 1) + dot(low, selector, 1, 1)

    share = emis_ref[...]
    emission = emission_ref[...]

    incoming = fwd_part[e]
    for k in range(1, emit_count):
        peer = partner(e, k, emit_count)
        arrival(fwd_got, fwd_send, fwd_recv, "emit", peer).wait_recv()
        incoming = incoming + fwd_got[peer]
    out_rad[...] = share * emission + (1.0 - share) * incoming
    stores[0].start()
    returned = adj_part[r]
    for k in range(1, recv_count):
        peer = partner(r, k, recv_count)
        arrival(adj_got, ret_send, ret_recv, "recv", peer).wait_recv()
        returned = returned + adj_got[peer]
    adjoint = source + returned
    out_adj[...] = adjoint
    stores[1].start()
    out_grad[...] = jnp.sum(adjoint * (emission - incoming), axis=0, keepdims=True)
    stores[2].start()

    for copy in row_geom_out + col_geom_out + val_out + wt_out + fwd_out + ret_out:
        copy.wait_send()
    for copy in stores:
        copy.wait()


def finish(rad_in, adj_in, grad_in, rad_out, adj_out, grad_out, rad, adj, grad, load_sem, store_sem):
    loads, stores = [], []
    for n, (src, held, dst) in enumerate(
        ((rad_in, rad, rad_out), (adj_in, adj, adj_out), (grad_in, grad, grad_out))
    ):
        loads.append(pltpu.make_async_copy(src, held, load_sem.at[n]))
        stores.append(pltpu.make_async_copy(held, dst, store_sem.at[n]))
    for load in loads:
        load.start()
    for load, store in zip(loads, stores):
        load.wait()
        store.start()
    for store in stores:
        store.wait()


def local(
    positions,
    angles,
    areas,
    emissivity,
    emission,
    radiosity_in,
    adjoint_in,
    visibility,
    inlet_patches,
    inlet_weights,
):
    emit_count = lax.axis_size("emit")
    recv_count = lax.axis_size("recv")
    own = areas.shape[0]
    cases = emission.shape[0]
    blocks = own // BLK
    row_total = own * recv_count
    group = math.gcd(recv_count, 4)
    hbm = pl.BlockSpec(memory_space=pltpu.HBM)
    emit_sem = pltpu.SemaphoreType.DMA((emit_count,))
    recv_sem = pltpu.SemaphoreType.DMA((recv_count,))
    operands = (
        positions,
        angles,
        areas[None, :],
        emissivity[None, :],
        radiosity_in,
        adjoint_in,
        visibility,
        inlet_patches[None, :],
        inlet_weights,
        emission,
    )
    flat = jax.ShapeDtypeStruct((cases, own), F32)
    results = (flat, flat, jax.ShapeDtypeStruct((1, own), F32))
    swept = pl.pallas_call(
        functools.partial(sweep, emit_count, recv_count),
        out_shape=results,
        in_specs=[hbm] * len(operands),
        out_specs=(hbm,) * 3,
        scratch_shapes=[pltpu.VMEM(x.shape, x.dtype) for x in operands]
        + [pltpu.VMEM(x.shape, x.dtype) for x in results]
        + [
            pltpu.SemaphoreType.DMA((len(operands),)),
            pltpu.SemaphoreType.DMA((3,)),
            pltpu.VMEM((recv_count, 8, own), F32),
            pltpu.VMEM((emit_count, 8, own), F32),
            pltpu.VMEM((recv_count, cases, own), BF16),
            pltpu.VMEM((emit_count, cases, own), BF16),
            pltpu.VMEM((emit_count * blocks, row_total), F32),
            pltpu.VMEM((recv_count, 48, own), BF16),
            pltpu.VMEM((recv_count, 48, own), BF16),
            pltpu.VMEM((recv_count, 48, own), BF16),
            pltpu.VMEM((own, own * group), BF16),
            pltpu.VMEM((row_total, cases), BF16),
            pltpu.VMEM((emit_count, cases, own), F32),
            pltpu.VMEM((emit_count, cases, own), F32),
            pltpu.VMEM((recv_count, cases, own), F32),
            pltpu.VMEM((recv_count, cases, own), F32),
            recv_sem,
            recv_sem,
            emit_sem,
            emit_sem,
            recv_sem,
            recv_sem,
            emit_sem,
            emit_sem,
            emit_sem,
            emit_sem,
            recv_sem,
            recv_sem,
        ],
        compiler_params=pltpu.CompilerParams(
            collective_id=0, has_side_effects=True, vmem_limit_bytes=64 * 1024 * 1024
        ),
        name="sweep",
    )(*operands)
    radiosity_out, adjoint_out, grad = pl.pallas_call(
        finish,
        out_shape=results,
        in_specs=[hbm] * 3,
        out_specs=(hbm,) * 3,
        scratch_shapes=[pltpu.VMEM(x.shape, x.dtype) for x in results]
        + [pltpu.SemaphoreType.DMA((3,)), pltpu.SemaphoreType.DMA((3,))],
        compiler_params=pltpu.CompilerParams(vmem_limit_bytes=64 * 1024 * 1024),
        name="finish",
    )(*swept)
    return (radiosity_out, adjoint_out, grad[0])


def solution(mesh):
    placed = (
        P(None, ("groups", "emit", "recv")),
        P(None, ("groups", "emit", "recv")),
        P(("groups", "emit", "recv")),
        P(("groups", "emit", "recv")),
        P(None, ("groups", "emit", "recv")),
        P(None, ("groups", "emit", "recv")),
        P(None, ("groups", "emit", "recv")),
        P(("groups", "emit"), None),
        P("groups"),
        P(None, "groups"),
    )
    return jax.shard_map(
        local,
        mesh=mesh,
        in_specs=placed,
        out_specs=(
            P(None, ("groups", "emit", "recv")),
            P(None, ("groups", "emit", "recv")),
            P(("groups", "emit", "recv")),
        ),
        check_vma=False,
    )
```
